512 devices in a mesh: pair: 8 (over x, core), role: 2 (over z_lo), shard: 32 (over z_hi, y).
Axes of the slice: x: 4, y: 8, z: 8 (z_hi: 4, z_lo: 2; z = z_hi * 2 + z_lo), core: 2. Of those that a mesh axis runs over, the one named last changes fastest.
Arguments:
- queries: bfloat16 [3072, 64, 128], P(('pair', 'role', 'shard')), parts along dimension 0, may hold values from -100 to 100
- cache_keys: bfloat16 [3072, 128, 512], P(('pair', 'role', 'shard')), parts along dimension 0, may hold values from -4 to 4
- cache_values: bfloat16 [3072, 128, 512], P(('pair', 'role', 'shard')), parts along dimension 0, may hold values from -6 to 6
- new_keys: bfloat16 [3072, 512], P(('pair', 'role', 'shard')), parts along dimension 0, may hold values from -6 to 6
- new_values: bfloat16 [3072, 512], P(('pair', 'role', 'shard')), parts along dimension 0, may hold values from -6 to 6
- lengths: int32 [3072], P(('pair', 'role', 'shard')), parts along dimension 0, may hold values from 1 to 128, 24576 in all
- residual: bfloat16 [3072, 8192], P(('pair', 'role', 'shard')), parts along dimension 0, may hold values from -6 to 6
- norm_gain: float32 [8192], replicated, may hold values from 0.1 to 1.9
- gate_weight: bfloat16 [8192, 4096], P('role', 'shard'), may hold values from -0.0625 to 0.0625
- up_weight: bfloat16 [8192, 4096], P('role', 'shard'), may hold values from -0.0625 to 0.0625
- down_weight: bfloat16 [4096, 8192], P('shard', 'role'), may hold values from -0.09375 to 0.09375
Outputs:
- layer_out: bfloat16 [3072, 8192], P(('pair', 'role', 'shard')), parts along dimension 0
The draws below stay inside these ranges and needn't reach their ends.
There are 8 independent parts, one for each index of `pair`. The reference program is written for one: setup_inputs(seed, part) draws one part's arguments, and reference() takes and returns one part's arrays. A program takes and returns all parts, laid end to end along the dimension named above; an argument that names none is the same for every part. Nothing has to cross between parts.
Inputs may be any that keep to these rules, and one draw needn't show every extreme that they name: `lengths`: some request has all 128 slots valid.
All inputs are finite; a program needn't handle non-finite values. No bound on the sum of `lengths` on one device may be relied on, other than what follows from the above.
Results may differ from the reference program's by a relative error of at most 0.02.
Values may be sent and summed in bfloat16 or wider, within the bound.
A program may use at most 64 MiB of HBM per device.

```python
import math
import jax
import jax.numpy as jnp
import numpy as np
from jax import lax

HD = 128
QH = 64
KVH = 4
FF_DEV = 128
LMAX = 128
D = 8192
FF = 4096
REQ = 384
N_SHARD = 32


def keys_base(key):
    return jax.random.truncated_normal(key, -4.0, 4.0, (REQ, LMAX, KVH * HD), jnp.float32)


def draw_cache_keys(key, part):
    base = keys_base(key)
    return base.astype(jnp.bfloat16)


def draw_queries(key, part):
    key = jax.random.fold_in(key, 5)
    fresh = jax.random.truncated_normal(key, -4.0, 4.0, (REQ, QH, HD), jnp.float32)
    return fresh.astype(jnp.bfloat16)


def steps_of(stream_key, shape, cuts, smallest, top_value):
    def one(axis_at, blocks):
        draws = jax.random.uniform(jax.random.fold_in(jax.random.fold_in(stream_key, 6), axis_at), (blocks,), jnp.float32, smallest / len(cuts), top_value / len(cuts))
        return jnp.repeat(jnp.exp(draws), shape[axis_at] // blocks).reshape((-1,) + (1,) * (len(shape) - axis_at - 1))

    gain = one(*cuts[0])
    for cut in cuts[1:]:
        gain = gain * one(*cut)
    return gain


def split_up(number_of, total, most, lean):
    loads = [(1 << 20) // math.isqrt(standing ** lean) + 1 for standing in range(2, number_of + 1)]
    rest, counts = total - most - (number_of - 1), [1] * (number_of - 1)
    while rest > 0:
        candidates = [i for i in range(number_of - 1) if counts[i] < most]
        pool, remaining = sum([loads[i] for i in candidates]), rest
        for i in candidates:
            addition = min(most - counts[i], max(1, remaining * loads[i] // pool), rest)
            counts[i] = counts[i] + addition
            rest = rest - addition
    return np.array([most] + counts)


def uneven_parts(rng, amount, total, reach, skew):
    if amount == 2:
        one = jax.random.randint(rng, (), max(1, total - reach), min(reach, total - 1) + 1)
        return jnp.stack([one, total - one])
    sizes = jnp.asarray(split_up(amount, total, reach, skew), jnp.int32)
    pairs = (amount - 1) // 2
    giver, taker = sizes[1:1 + 2 * pairs:2], sizes[2:2 + 2 * pairs:2]
    margin = jnp.minimum(giver - 1, reach - taker)
    passed = jax.random.randint(jax.random.fold_in(rng, 1), (pairs,), 0, 1 << 20) % (margin + 1)
    sizes = sizes.at[1:1 + 2 * pairs:2].set(giver - passed).at[2:2 + 2 * pairs:2].set(taker + passed)
    return sizes[jax.random.permutation(jax.random.fold_in(rng, 2), amount)]


def centred(rng, shape, spread, most, split=(), kind=jnp.bfloat16):
    factor_of = steps_of(rng, shape, split, -0.22, 0.18) if split else 1.0
    drawn = jax.random.normal(rng, shape, jnp.float32) * spread * factor_of
    return jnp.minimum(jnp.maximum(drawn, -most), most).astype(kind)


def setup_inputs(seed: int = 0, part: int = 0) -> dict:
    key_list = jax.random.split(jax.random.key(seed), 12)
    part_splits = jax.random.split(jax.random.fold_in(key_list[11], part), 12)
    queries = draw_queries(jax.random.fold_in(jax.random.fold_in(key_list[11], part), 71), part)
    cache_keys = draw_cache_keys(jax.random.fold_in(jax.random.fold_in(key_list[11], part), 71), part)
    cache_values = centred(part_splits[2], (REQ, LMAX, KVH * HD), 1.0, 6.0, ((0, 64),))
    new_keys = centred(part_splits[3], (REQ, KVH * HD), 1.0, 6.0, ((0, 64),))
    new_values = centred(part_splits[4], (REQ, KVH * HD), 1.0, 6.0, ((0, 64),))
    lengths = uneven_parts(part_splits[5], REQ, REQ * LMAX // 2, LMAX, 2).astype(jnp.int32)
    residual = centred(part_splits[6], (REQ, D), 1.0, 6.0, ((0, 64),))
    norm_gain = jnp.clip(1.0 + 0.18 * jax.random.normal(key_list[7], (D,), jnp.float32), 0.1, 1.9)
    gate_weight = centred(key_list[8], (D, FF), D ** -0.5, 0.0625, ((0, 2), (1, 32)))
    up_weight = centred(key_list[9], (D, FF), D ** -0.5, 0.0625, ((0, 2), (1, 32)))
    down_weight = centred(key_list[10], (FF, D), FF ** -0.5, 0.09375, ((0, 32), (1, 2)))
    return {"queries": queries, "cache_keys": cache_keys, "cache_values": cache_values, "new_keys": new_keys, "new_values": new_values, "lengths": lengths, "residual": residual, "norm_gain": norm_gain, "gate_weight": gate_weight, "up_weight": up_weight, "down_weight": down_weight}


def attend_one(args):
    query, keys, values, new_key, new_value, length = args
    groups = QH // KVH
    grouped = query.astype(jnp.float32).reshape(KVH, groups, HD)
    keys_four = keys.astype(jnp.float32).reshape(LMAX, KVH, HD)
    values_four = values.astype(jnp.float32).reshape(LMAX, KVH, HD)
    new_key_two = new_key.astype(jnp.float32).reshape(KVH, HD)
    new_value_two = new_value.astype(jnp.float32).reshape(KVH, HD)
    scale = 1.0 / jnp.sqrt(jnp.float32(HD))
    scores = jnp.einsum('kgd,lkd->kgl', grouped, keys_four) * scale
    own = jnp.einsum('kgd,kd->kg', grouped, new_key_two) * scale
    valid = jnp.arange(LMAX) < length
    scores = jnp.where(valid[None, None, :], scores, jnp.float32(-1e+30))
    top = jnp.maximum(lax.optimization_barrier(jnp.max(scores, axis=-1)), own)
    weights = jnp.where(valid[None, None, :], jnp.exp(scores - top[..., None]), jnp.float32(0.0))
    own_weight = jnp.exp(own - top)
    total = lax.optimization_barrier(jnp.sum(weights, axis=-1)) + own_weight
    weights_low = weights.astype(jnp.bfloat16).astype(jnp.float32)
    own_low = own_weight.astype(jnp.bfloat16).astype(jnp.float32)
    summed = jnp.einsum('kgl,lkd->kgd', weights_low, values_four)
    summed = summed + own_low[..., None] * new_value_two[:, None, :]
    return (summed / total[..., None]).reshape(QH * HD)

def reference(queries, cache_keys, cache_values, new_keys, new_values, lengths, residual, norm_gain, gate_weight, up_weight, down_weight):
    attended = lax.map(attend_one, (queries, cache_keys, cache_values, new_keys, new_values, lengths))
    mixed = residual.astype(jnp.float32) + attended
    scale = lax.rsqrt(lax.optimization_barrier(jnp.mean(mixed * mixed, axis=-1, keepdims=True)) + 1e-05)
    normed = (mixed * scale * norm_gain[None, :]).astype(jnp.bfloat16)
    gate = jnp.dot(normed, gate_weight, preferred_element_type=jnp.float32)
    up = jnp.dot(normed, up_weight, preferred_element_type=jnp.float32)
    hidden = (jax.nn.silu(gate) * up).astype(jnp.bfloat16)
    blocks = hidden.reshape(REQ, N_SHARD, FF_DEV).transpose(1, 0, 2)
    down_blocks = down_weight.reshape(N_SHARD, FF_DEV, D)

    def add_block(total, pieces):
        term = jnp.dot(pieces[0], pieces[1], preferred_element_type=jnp.float32)
        return (total + term.astype(jnp.bfloat16).astype(jnp.float32), None)
    feed, unused = lax.scan(add_block, jnp.zeros((REQ, D), jnp.float32), (blocks, down_blocks))
    return (mixed + feed).astype(jnp.bfloat16)
```

```python
import jax
import jax.numpy as jnp
from jax import lax
from jax.experimental import pallas as pl
from jax.experimental.pallas import tpu as pltpu
from jax.sharding import PartitionSpec as P

MESH = pl.DeviceIdType.MESH
F32 = jnp.float32
BF16 = jnp.bfloat16
R = 6
HD = 128
QH = 64
KVH = 4
GRP = QH // KVH
L = 128
N = 8
ROWS = R * N
FB = 1024
HB = 128
NB = 4
HALF = FB // 2


def mod(a, n):
    return lax.rem(a + 4 * n, n)


def kernel(
    q_ref, nk_ref, nv_ref, len_ref, res_ref, gain_ref, ck_hbm, cv_hbm, gate_hbm, up_hbm, down_hbm,
    out_ref,
    ck, cv, wgu, wd, scores, mixed, natural, n_send, n_recv, relay, acts, rz_send, rz_recv, hid, ry_send, ry_recv,
    f_send, f_recv,
    cache_sem, own_sem, wz_ssem, wz_rsem, wx_ssem, wx_rsem, wc_ssem, wc_rsem, a1_ssem, a1_rsem, ag_ssem, ag_rsem,
    rz_ssem, rz_rsem, hg_ssem, hg_rsem, ry_ssem, ry_rsem, a2_ssem, a2_rsem,
):
    pair, role, shard = lax.axis_index("pair"), lax.axis_index("role"), lax.axis_index("shard")
    x, c = pair // 2, lax.rem(pair, 2)
    z_hi, y = shard // 8, lax.rem(shard, 8)
    z = z_hi * 2 + role

    def at_z(k):
        to = mod(z + k, 8)
        return (pair, lax.rem(to, 2), (to // 2) * 8 + y)

    def at_y(k):
        return (pair, role, z_hi * 8 + mod(y + k, 8))

    def at_x(k):
        return (mod(x + k, 4) * 2 + c, role, shard)

    sibling = (x * 2 + (1 - c), role, shard)

    sends = []

    def push(src, dst, ssem, rsem, to):
        copy = pltpu.make_async_remote_copy(
            src_ref=src, dst_ref=dst, send_sem=ssem, recv_sem=rsem, device_id=to, device_id_type=MESH
        )
        copy.start()
        sends.append(copy)
        return copy

    locals_ = []
    for i, (src, dst) in enumerate(((ck_hbm, ck), (cv_hbm, cv))):
        copy = pltpu.make_async_copy(src, dst, cache_sem.at[i])
        copy.start()
        locals_.append(copy)
    quarter = pl.ds(pl.multiple_of(z_hi * FB, FB), FB)
    own = []
    for i, (src, dst) in enumerate((
        (gate_hbm.at[quarter, :], wgu.at[0, :, pl.ds(0, HB)]),
        (up_hbm.at[quarter, :], wgu.at[0, :, pl.ds(HB, HB)]),
        (down_hbm.at[:, quarter], wd.at[0]),
    )):
        copy = pltpu.make_async_copy(src, dst, own_sem.at[i])
        copy.start()
        own.append(copy)

    barrier = pltpu.get_barrier_semaphore()
    partners = [at_z(k) for k in range(1, 8)] + [at_y(1), at_y(-1)] + [at_x(k) for k in range(1, 4)] + [sibling]
    for to in partners:
        pl.semaphore_signal(barrier, inc=1, device_id=to, device_id_type=MESH)
    pl.semaphore_wait(barrier, len(partners))

    p = c * 4 + x
    p_gu = pl.ds(pl.multiple_of(p * 128, 128), 128)
    p_d = pl.ds(pl.multiple_of(p * 16, 16), 16)
    wz = []
    for k in (1, 3, 2):
        q_to = mod(z_hi + k, 4)
        rows = pl.ds(pl.multiple_of(q_to * FB + p * 128, 128), 128)
        cols = pl.ds(pl.multiple_of(q_to * FB, FB), FB)
        to = (pair, role, q_to * 8 + y)
        for i, (src, dst) in enumerate((
            (gate_hbm.at[rows, :], wgu.at[4 - k, p_gu, pl.ds(0, HB)]),
            (up_hbm.at[rows, :], wgu.at[4 - k, p_gu, pl.ds(HB, HB)]),
            (down_hbm.at[p_d, cols], wd.at[4 - k, p_d, :]),
        )):
            wz.append((i, push(src, dst, wz_ssem.at[k - 1, i], wz_rsem.at[k - 1, i], to)))

    locals_[0].wait()
    for r in range(R):
        for k in range(KVH):
            scores[pl.ds(QH * r + GRP * k, GRP), :] = lax.dot_general(
                q_ref[r, pl.ds(GRP * k, GRP), :], ck[r, :, pl.ds(HD * k, HD)],
                (((1,), (1,)), ((), ())), preferred_element_type=F32,
            )

    for i, copy in wz:
        if i < 2:
            copy.wait_recv()
    part_gu = wgu.at[pl.ds(1, 3), p_gu, :]
    part_d = wd.at[pl.ds(1, 3), p_d, :]
    wx_gu = [push(part_gu, part_gu, wx_ssem.at[k - 1, 0], wx_rsem.at[k - 1, 0], at_x(k)) for k in (1, 3, 2)]

    for i in range(QH):
        mixed[pl.ds(i, R, stride=QH), :] = res_ref[:, pl.ds(HD * i, HD)].astype(F32)
    locals_[1].wait()
    scale = F32(1.0) / jnp.sqrt(F32(HD))
    slot = lax.broadcasted_iota(jnp.int32, (QH, L), 1)
    for r in range(R):
        rows = pl.ds(QH * r, QH)
        keys = [jnp.broadcast_to(nk_ref[pl.ds(r, 1), pl.ds(HD * k, HD)].astype(F32), (GRP, HD)) for k in range(KVH)]
        vals = [jnp.broadcast_to(nv_ref[pl.ds(r, 1), pl.ds(HD * k, HD)].astype(F32), (GRP, HD)) for k in range(KVH)]
        own_score = jnp.sum(q_ref[r].astype(F32) * jnp.concatenate(keys, 0), axis=1, keepdims=True) * scale
        valid = slot < len_ref[r]
        kept = jnp.where(valid, scores[rows, :] * scale, F32(-1e30))
        top = jnp.maximum(jnp.max(kept, axis=1, keepdims=True), own_score)
        weights = jnp.where(valid, jnp.exp(kept - top), F32(0.0))
        own_weight = jnp.exp(own_score - top)
        total = jnp.sum(weights, axis=1, keepdims=True) + own_weight
        low = weights.astype(BF16)
        summed = jnp.concatenate(
            [
                jnp.dot(low[GRP * k:GRP * (k + 1)], cv[r, :, pl.ds(HD * k, HD)], preferred_element_type=F32)
                for k in range(KVH)
            ], 0,
        )
        summed = summed + own_weight.astype(BF16).astype(F32) * jnp.concatenate(vals, 0)
        mix = mixed[rows, :] + summed / total
        mixed[rows, :] = mix
        mean = jnp.sum(jnp.sum(mix * mix, axis=1, keepdims=True), axis=0, keepdims=True) * F32(1.0 / (QH * HD))
        natural[rows, :] = mix * lax.rsqrt(mean + F32(1e-5)) * gain_ref[...]

    for e in range(N):
        n_send[e] = jnp.concatenate([natural[pl.ds(QH * r + 8 * e, 8), :] for r in range(R)], 0).astype(BF16)

    def tile_of(at):
        return lax.rem(at, 2) * 4 + at // 2

    a1 = [
        push(n_send.at[tile_of(mod(z + k, 8))], n_recv.at[z], a1_ssem.at[k - 1], a1_rsem.at[k - 1], at_z(k))
        for k in (4, 3, 5, 2, 6, 1, 7)
    ]
    n_recv[z] = n_send[tile_of(z)]
    for copy in a1:
        copy.wait_recv()
    relay[...] = n_recv[...].reshape(N * ROWS, HD).astype(F32)
    acts[y] = jnp.concatenate([relay[pl.ds(i, ROWS, stride=8), :] for i in range(8)], 1).astype(BF16)

    def gather(buf, me, at, ssem, rsem, width, between):
        half = width // 2
        arrivals = {}
        for t in range(4):
            for s in range(2):
                for way, sign in ((0, 1), (1, -1)):
                    if t:
                        arrivals[way, t - 1, s].wait_recv()
                    if t == 3 and s != way:
                        continue
                    ref = buf.at[mod(me - sign * t, 8), :, pl.ds(s * half, half)]
                    arrivals[way, t, s] = push(ref, ref, ssem.at[way, t, s], rsem.at[way, t, s], at(sign))
            between(t)
        for way in range(2):
            arrivals[way, 3, way].wait_recv()

    def scatter(term, me, at, ssem, rsem, sbuf, rbuf, between):
        arrivals = {}
        for t in range(4):
            for way, sign in ((0, 1), (1, -1)):
                target = mod(me + sign * (4 - t), 8)
                for s in range(2):
                    cols = pl.ds(s * HALF, HALF)
                    if t == 0 and s != way:
                        continue
                    value = term(target, s)
                    if (way, t - 1, s) in arrivals:
                        arrivals[way, t - 1, s].wait_recv()
                        value = value + rbuf[way, t - 1, :, cols].astype(F32)
                    sbuf[way, t, :, cols] = value.astype(BF16)
                    arrivals[way, t, s] = push(
                        sbuf.at[way, t, :, cols], rbuf.at[way, t, :, cols],
                        ssem.at[way, t, s], rsem.at[way, t, s], at(sign),
                    )
            between(t)
        out = []
        for s in range(2):
            cols = pl.ds(s * HALF, HALF)
            value = term(me, s)
            for way in range(2):
                arrivals[way, 3, s].wait_recv()
                value = value + rbuf[way, 3, :, cols].astype(F32)
            out.append(value)
        return out

    wx_d, wc = [], []

    def pass_weights(t):
        if t == 0:
            for i, copy in wz:
                if i == 2:
                    copy.wait_recv()
            wx_d.extend(push(part_d, part_d, wx_ssem.at[k - 1, 1], wx_rsem.at[k - 1, 1], at_x(k)) for k in (1, 3, 2))
        if t == 2:
            for copy in wx_gu:
                copy.wait_recv()
            ref = wgu.at[pl.ds(1, 3), pl.ds(pl.multiple_of(c * 512, 512), 512), :]
            wc.append(push(ref, ref, wc_ssem.at[0], wc_rsem.at[0], sibling))

    gather(acts, y, at_y, ag_ssem, ag_rsem, FB, pass_weights)
    own[0].wait()
    own[1].wait()
    wc[0].wait_recv()

    def gate_up(target, s):
        rows = acts[target]
        return jnp.concatenate(
            [
                jnp.dot(rows, wgu[mod(b - z_hi, 4)], preferred_element_type=F32)
                for b in (2 * s, 2 * s + 1)
            ], 1,
        )

    def pass_down(t):
        if t == 0:
            for copy in wx_d:
                copy.wait_recv()
            ref = wd.at[pl.ds(1, 3), pl.ds(pl.multiple_of(c * 64, 64), 64), :]
            wc.append(push(ref, ref, wc_ssem.at[1], wc_rsem.at[1], sibling))

    both = scatter(gate_up, z, at_z, rz_ssem, rz_rsem, rz_send, rz_recv, pass_down)
    hidden = []
    for s in range(2):
        for b in range(2):
            gate = both[s][:, 256 * b:256 * b + HB]
            up = both[s][:, 256 * b + HB:256 * (b + 1)]
            hidden.append((gate / (F32(1.0) + jnp.exp(-gate)) * up).astype(BF16))
    hid[z] = jnp.concatenate(hidden, 1)

    gather(hid, z, at_z, hg_ssem, hg_rsem, NB * HB, lambda t: None)
    own[2].wait()
    wc[1].wait_recv()

    def down_term(target, s):
        rows = hid[target]
        total = None
        for b in range(NB):
            term = jnp.dot(
                rows[:, HB * b:HB * (b + 1)], wd[mod(b - z_hi, 4), :, pl.ds(s * HALF, HALF)], preferred_element_type=F32
            )
            total = term if total is None else total + term
        return total

    feed = scatter(down_term, y, at_y, ry_ssem, ry_rsem, ry_send, ry_recv, lambda t: None)
    feed = jnp.concatenate(feed, 1)
    for i in range(8):
        relay[pl.ds(i, ROWS, stride=8), :] = feed[:, HD * i:HD * (i + 1)]
    f_send[...] = relay[...].astype(BF16).reshape(N, ROWS, HD)
    me = tile_of(z)
    a2 = [
        push(f_send.at[mod(z + k, 8)], f_recv.at[me], a2_ssem.at[k - 1], a2_rsem.at[k - 1], at_z(k))
        for k in (4, 3, 5, 2, 6, 1, 7)
    ]
    f_recv[me] = f_send[z]
    for copy in a2:
        copy.wait_recv()
    for e in range(N):
        mix = jnp.concatenate([mixed[pl.ds(QH * r + 8 * e, 8), :] for r in range(R)], 0)
        natural[pl.ds(ROWS * e, ROWS), :] = mix + f_recv[e].astype(F32)
    for e in range(N):
        for i in range(8):
            out_ref[:, pl.ds(FB * e + HD * i, HD)] = natural[pl.ds(ROWS * e + i, R, stride=8), :].astype(BF16)
    for copy in sends:
        copy.wait_send()


def per_device(q, ck, cv, nk, nv, lengths, residual, gain, gate, up, down):
    vmem = pl.BlockSpec(memory_space=pltpu.VMEM)
    smem = pl.BlockSpec(memory_space=pltpu.SMEM)
    hbm = pl.BlockSpec(memory_space=pl.ANY)
    dma = pltpu.SemaphoreType.DMA
    ring = (2, 4, 2)
    return pl.pallas_call(
        kernel,
        out_shape=jax.ShapeDtypeStruct((R, QH * HD), BF16),
        in_specs=[vmem, vmem, vmem, smem, vmem, vmem, hbm, hbm, hbm, hbm, hbm],
        out_specs=vmem,
        scratch_shapes=[
            pltpu.VMEM((R, L, KVH * HD), BF16),
            pltpu.VMEM((R, L, KVH * HD), BF16),
            pltpu.VMEM((NB, FB, 2 * HB), BF16),
            pltpu.VMEM((NB, HB, FB), BF16),
            pltpu.VMEM((R * QH, L), F32),
            pltpu.VMEM((R * QH, HD), F32),
            pltpu.VMEM((R * QH, HD), F32),
            pltpu.VMEM((N, ROWS, HD), BF16),
            pltpu.VMEM((N, ROWS, HD), BF16),
            pltpu.VMEM((N * ROWS, HD), F32),
            pltpu.VMEM((N, ROWS, FB), BF16),
            pltpu.VMEM((2, 4, ROWS, FB), BF16),
            pltpu.VMEM((2, 4, ROWS, FB), BF16),
            pltpu.VMEM((N, ROWS, NB * HB), BF16),
            pltpu.VMEM((2, 4, ROWS, FB), BF16),
            pltpu.VMEM((2, 4, ROWS, FB), BF16),
            pltpu.VMEM((N, ROWS, HD), BF16),
            pltpu.VMEM((N, ROWS, HD), BF16),
            dma((2,)), dma((3,)),
            dma((3, 3)), dma((3, 3)),
            dma((3, 2)), dma((3, 2)),
            dma((2,)), dma((2,)),
            dma((7,)), dma((7,)),
            dma(ring), dma(ring),
            dma(ring), dma(ring),
            dma(ring), dma(ring),
            dma(ring), dma(ring),
            dma((7,)), dma((7,)),
        ],
        compiler_params=pltpu.CompilerParams(
            collective_id=0, has_side_effects=True, vmem_limit_bytes=48 * 1024 * 1024
        ),
        cost_estimate=pl.CostEstimate(flops=1_400_000_000, bytes_accessed=5_000_000, transcendentals=100_000),
    )(q, nk, nv, lengths, residual, gain.reshape(QH, HD), ck, cv, gate, up, down)


def solution(mesh):
    rows = ("pair", "role", "shard")
    return jax.shard_map(
        per_device,
        mesh=mesh,
        in_specs=(
            P(rows, None, None), P(rows, None, None), P(rows, None, None), P(rows, None), P(rows, None), P(rows),
            P(rows, None), P(), P("role", "shard"), P("role", "shard"), P("shard", "role"),
        ),
        out_specs=P(rows, None),
        check_vma=False,
    )
```

```python
import jax
import jax.numpy as jnp
from jax import lax
from jax.experimental import pallas as pl
from jax.experimental.pallas import tpu as pltpu
from jax.sharding import PartitionSpec as P

MESH = pl.DeviceIdType.MESH
F32 = jnp.float32
BF16 = jnp.bfloat16
R = 6
HD = 128
QH = 64
KVH = 4
GRP = QH // KVH
L = 128
N = 8
ROWS = R * N
FB = 1024
HB = 128
NB = 4
HALF = FB // 2


def mod(a, n):
    return lax.rem(a + 4 * n, n)


def kernel(
    len_ref, q_hbm, ck_hbm, cv_hbm, nk_hbm, nv_hbm, res_hbm, gain_hbm, gate_hbm, up_hbm, down_hbm,
    out_ref,
    q_ref, ck, cv, nk_ref, nv_ref, res_ref, gain_ref, wgu, wd, scores, mixed, natural, n_send, n_recv, relay,
    acts, rz_send, rz_recv, hid, ry_send, ry_recv, f_send, f_recv,
    local_sem, own_sem, wz_ssem, wz_rsem, wx_ssem, wx_rsem, wc_ssem, wc_rsem, ready_sem, a1_ssem, a1_rsem, ag_ssem, ag_rsem,
    rz_ssem, rz_rsem, hg_ssem, hg_rsem, ry_ssem, ry_rsem, a2_ssem, a2_rsem,
):
    pair, role, shard = lax.axis_index("pair"), lax.axis_index("role"), lax.axis_index("shard")
    x, c = pair // 2, lax.rem(pair, 2)
    z_hi, y = shard // 8, lax.rem(shard, 8)
    z = z_hi * 2 + role

    def at_z(k):
        to = mod(z + k, 8)
        return (pair, lax.rem(to, 2), (to // 2) * 8 + y)

    def at_y(k):
        return (pair, role, z_hi * 8 + mod(y + k, 8))

    def at_x(k):
        return (mod(x + k, 4) * 2 + c, role, shard)

    sibling = (x * 2 + (1 - c), role, shard)

    def remote(src, dst, ssem, rsem, to):
        return pltpu.make_async_remote_copy(
            src_ref=src, dst_ref=dst, send_sem=ssem, recv_sem=rsem, device_id=to, device_id_type=MESH
        )

    operands = []
    for i, (src, dst) in enumerate((
        (q_hbm, q_ref), (ck_hbm, ck), (cv_hbm, cv), (nk_hbm, nk_ref), (nv_hbm, nv_ref), (res_hbm, res_ref), (gain_hbm, gain_ref),
    )):
        copy = pltpu.make_async_copy(src, dst, local_sem.at[i])
        copy.start()
        operands.append(copy)
    quarter = pl.ds(pl.multiple_of(z_hi * FB, FB), FB)
    own = []
    for i, (src, dst) in enumerate((
        (gate_hbm.at[quarter, :], wgu.at[0, :, pl.ds(0, HB)]),
        (up_hbm.at[quarter, :], wgu.at[0, :, pl.ds(HB, HB)]),
        (down_hbm.at[:, quarter], wd.at[0]),
    )):
        copy = pltpu.make_async_copy(src, dst, own_sem.at[i])
        copy.start()
        own.append(copy)

    barrier = pltpu.get_barrier_semaphore()

    def greet(to):
        pl.semaphore_signal(barrier, inc=1, device_id=to, device_id_type=MESH)

    for k in range(1, 8):
        greet(at_z(k))
        greet(at_y(k))

    @pl.when(c == 0)
    def _():
        for k in range(1, 4):
            greet(at_x(k))
        greet(sibling)
        pl.semaphore_wait(barrier, 17)

    @pl.when(c == 1)
    def _():
        pl.semaphore_wait(barrier, 15)
        pl.semaphore_signal(ready_sem, inc=1, device_id=sibling, device_id_type=MESH)

    part = pl.ds(pl.multiple_of(x * 256, 256), 256)
    part_d = pl.ds(pl.multiple_of(x * 32, 32), 32)

    def weight_z(k, i):
        q_to = mod(z_hi + k, 4)
        rows = pl.ds(pl.multiple_of(q_to * FB + x * 256, 256), 256)
        cols = pl.ds(pl.multiple_of(q_to * FB, FB), FB)
        src, dst = (
            (gate_hbm.at[rows, :], wgu.at[4 - k, part, pl.ds(0, HB)]),
            (up_hbm.at[rows, :], wgu.at[4 - k, part, pl.ds(HB, HB)]),
            (down_hbm.at[part_d, cols], wd.at[4 - k, part_d, :]),
        )[i]
        return remote(src, dst, wz_ssem.at[k - 1, i], wz_rsem.at[k - 1, i], (pair, role, q_to * 8 + y))

    def weight_x(k, to, i):
        ref = (wgu.at[4 - k, part, :], wd.at[4 - k, part_d, :])[i]
        return remote(ref, ref, wx_ssem.at[k - 1, to - 1, i], wx_rsem.at[k - 1, to - 1, i], at_x(to))

    def weight_c(i):
        ref = (wgu, wd)[i].at[pl.ds(1, 3)]
        return remote(ref, ref, wc_ssem.at[i], wc_rsem.at[i], sibling)

    @pl.when(c == 0)
    def _():
        for k in (1, 3, 2):
            weight_z(k, 0).start()
            weight_z(k, 1).start()

    def pass_gate_up(k):
        @pl.when(c == 0)
        def _():
            weight_z(k, 0).wait_recv()
            weight_z(k, 1).wait_recv()
            for to in (2, 1, 3):
                weight_x(k, to, 0).start()

    for copy in operands[:2]:
        copy.wait()
    for r in range(R):
        for k in range(KVH):
            scores[pl.ds(QH * r + GRP * k, GRP), :] = lax.dot_general(
                q_ref[r, pl.ds(GRP * k, GRP), :], ck[r, :, pl.ds(HD * k, HD)],
                (((1,), (1,)), ((), ())), preferred_element_type=F32,
            )
    for copy in operands[2:]:
        copy.wait()
    for i in range(QH):
        mixed[pl.ds(i, R, stride=QH), :] = res_ref[:, pl.ds(HD * i, HD)].astype(F32)
    scale = F32(1.0) / jnp.sqrt(F32(HD))
    slot = lax.broadcasted_iota(jnp.int32, (QH, L), 1)
    for r in range(R):
        if r in (2, 3, 4):
            pass_gate_up((1, 3, 2)[r - 2])
        rows = pl.ds(QH * r, QH)
        keys = [jnp.broadcast_to(nk_ref[pl.ds(r, 1), pl.ds(HD * k, HD)].astype(F32), (GRP, HD)) for k in range(KVH)]
        vals = [jnp.broadcast_to(nv_ref[pl.ds(r, 1), pl.ds(HD * k, HD)].astype(F32), (GRP, HD)) for k in range(KVH)]
        own_score = jnp.sum(q_ref[r].astype(F32) * jnp.concatenate(keys, 0), axis=1, keepdims=True) * scale
        valid = slot < len_ref[r]
        kept = jnp.where(valid, scores[rows, :] * scale, F32(-1e30))
        top = jnp.maximum(jnp.max(kept, axis=1, keepdims=True), own_score)
        weights = jnp.where(valid, jnp.exp(kept - top), F32(0.0))
        own_weight = jnp.exp(own_score - top)
        total = jnp.sum(weights, axis=1, keepdims=True) + own_weight
        low = weights.astype(BF16)
        summed = jnp.concatenate(
            [
                jnp.dot(low[GRP * k:GRP * (k + 1)], cv[r, :, pl.ds(HD * k, HD)], preferred_element_type=F32)
                for k in range(KVH)
            ], 0,
        )
        summed = summed + own_weight.astype(BF16).astype(F32) * jnp.concatenate(vals, 0)
        mix = mixed[rows, :] + summed / total
        mixed[rows, :] = mix
        mean = jnp.sum(jnp.sum(mix * mix, axis=1, keepdims=True), axis=0, keepdims=True) * F32(1.0 / (QH * HD))
        natural[rows, :] = mix * lax.rsqrt(mean + F32(1e-5)) * gain_ref[...]

    for e in range(N):
        n_send[e] = jnp.concatenate([natural[pl.ds(QH * r + 8 * e, 8), :] for r in range(R)], 0).astype(BF16)

    def tile_of(at):
        return lax.rem(at, 2) * 4 + at // 2

    far_first = (4, 3, 5, 2, 6, 1, 7)
    near_first = (1, 7, 2, 6, 3, 5, 4)
    a1 = [
        remote(n_send.at[tile_of(mod(z + k, 8))], n_recv.at[z], a1_ssem.at[k - 1], a1_rsem.at[k - 1], at_z(k))
        for k in far_first
    ]
    for copy in a1:
        copy.start()
    n_recv[z] = n_send[tile_of(z)]

    @pl.when(c == 0)
    def _():
        for k in (1, 3, 2):
            weight_z(k, 2).start()

    for copy in a1:
        copy.wait_recv()
    relay[...] = n_recv[...].reshape(N * ROWS, HD).astype(F32)
    acts[0] = jnp.concatenate([relay[pl.ds(i, ROWS, stride=8), :] for i in range(8)], 1).astype(BF16)

    ag = {k: remote(acts.at[0], acts.at[k], ag_ssem.at[k - 1], ag_rsem.at[k - 1], at_y(k)) for k in far_first}
    for k in far_first:
        ag[k].start()

    @pl.when(c == 0)
    def _():
        for k in (1, 3, 2):
            weight_z(k, 2).wait_recv()
            for to in (2, 1, 3):
                weight_x(k, to, 1).start()
        for k in (1, 3, 2):
            for to in (2, 1, 3):
                weight_x(k, to, 0).wait_recv()

    @pl.when(c == 1)
    def _():
        weight_c(0).wait_recv()

    own[0].wait()
    own[1].wait()

    def rz(k):
        return remote(rz_send.at[k], rz_recv.at[k], rz_ssem.at[k], rz_rsem.at[k], at_z(k))

    for n, k in enumerate((0,) + near_first):
        if k:
            ag[k].wait_recv()
        to = mod(y - k - z, 8)
        rows = acts[k]
        for b in range(NB):
            rz_send[to, :, pl.ds(2 * HB * b, 2 * HB)] = jnp.dot(
                rows, wgu[mod(b - z_hi, 4)], preferred_element_type=F32
            ).astype(BF16)

        @pl.when(to != 0)
        def _(to=to):
            rz(to).start()

        if n == 4:
            @pl.when(c == 0)
            def _():
                pl.semaphore_wait(ready_sem, 1)
                weight_c(0).start()

    for k in near_first:
        rz(k).wait_recv()
    for b in range(NB):
        cols = pl.ds(2 * HB * b, 2 * HB)
        both = rz_send[0, :, cols].astype(F32)
        for k in range(1, 8):
            both = both + rz_recv[k, :, cols].astype(F32)
        gate, up = both[:, :HB], both[:, HB:]
        hid[0, :, pl.ds(HB * b, HB)] = (gate / (F32(1.0) + jnp.exp(-gate)) * up).astype(BF16)

    hg = {k: remote(hid.at[0], hid.at[k], hg_ssem.at[k - 1], hg_rsem.at[k - 1], at_z(k)) for k in far_first}
    for k in far_first:
        hg[k].start()

    @pl.when(c == 0)
    def _():
        for k in (1, 3, 2):
            for to in (2, 1, 3):
                weight_x(k, to, 1).wait_recv()

    own[2].wait()

    @pl.when(c == 0)
    def _():
        weight_c(1).start()

    @pl.when(c == 1)
    def _():
        weight_c(1).wait_recv()

    def ry(k):
        return remote(ry_send.at[k], ry_recv.at[k], ry_ssem.at[k], ry_rsem.at[k], at_y(k))

    for k in (0,) + near_first:
        if k:
            hg[k].wait_recv()
        to = mod(z - k - y, 8)
        total = None
        for b in range(NB):
            term = jnp.dot(hid[k, :, pl.ds(HB * b, HB)], wd[mod(b - z_hi, 4)], preferred_element_type=F32)
            total = term if total is None else total + term
        ry_send[to] = total.astype(BF16)

        @pl.when(to != 0)
        def _(to=to):
            ry(to).start()

    for k in near_first:
        ry(k).wait_recv()
    for i in range(8):
        cols = pl.ds(HD * i, HD)
        feed = ry_send[0, :, cols].astype(F32)
        for k in range(1, 8):
            feed = feed + ry_recv[k, :, cols].astype(F32)
        relay[pl.ds(i, ROWS, stride=8), :] = feed
    f_send[...] = relay[...].astype(BF16).reshape(N, ROWS, HD)

    me = tile_of(z)
    a2 = [
        remote(f_send.at[mod(z + k, 8)], f_recv.at[me], a2_ssem.at[k - 1], a2_rsem.at[k - 1], at_z(k)) for k in far_first
    ]
    for copy in a2:
        copy.start()
    f_recv[me] = f_send[z]
    for copy in a2:
        copy.wait_recv()
    for e in range(N):
        mix = jnp.concatenate([mixed[pl.ds(QH * r + 8 * e, 8), :] for r in range(R)], 0)
        natural[pl.ds(ROWS * e, ROWS), :] = mix + f_recv[e].astype(F32)
    for e in range(N):
        for i in range(8):
            out_ref[:, pl.ds(FB * e + HD * i, HD)] = natural[pl.ds(ROWS * e + i, R, stride=8), :].astype(BF16)

    for copy in a1 + a2 + list(ag.values()) + list(hg.values()):
        copy.wait_send()
    for k in far_first:
        rz(k).wait_send()
        ry(k).wait_send()

    @pl.when(c == 0)
    def _():
        for k in (1, 2, 3):
            for i in range(3):
                weight_z(k, i).wait_send()
            for to in (1, 2, 3):
                for i in range(2):
                    weight_x(k, to, i).wait_send()
        for i in range(2):
            weight_c(i).wait_send()


def per_device(q, ck, cv, nk, nv, lengths, residual, gain, gate, up, down):
    vmem = pl.BlockSpec(memory_space=pltpu.VMEM)
    smem = pl.BlockSpec(memory_space=pltpu.SMEM)
    hbm = pl.BlockSpec(memory_space=pl.ANY)
    dma = pltpu.SemaphoreType.DMA
    return pl.pallas_call(
        kernel,
        out_shape=jax.ShapeDtypeStruct((R, QH * HD), BF16),
        in_specs=[smem] + [hbm] * 10,
        out_specs=vmem,
        scratch_shapes=[
            pltpu.VMEM((R, QH, HD), BF16),
            pltpu.VMEM((R, L, KVH * HD), BF16),
            pltpu.VMEM((R, L, KVH * HD), BF16),
            pltpu.VMEM((R, KVH * HD), BF16),
            pltpu.VMEM((R, KVH * HD), BF16),
            pltpu.VMEM((R, QH * HD), BF16),
            pltpu.VMEM((QH, HD), F32),
            pltpu.VMEM((NB, FB, 2 * HB), BF16),
            pltpu.VMEM((NB, HB, FB), BF16),
            pltpu.VMEM((R * QH, L), F32),
            pltpu.VMEM((R * QH, HD), F32),
            pltpu.VMEM((R * QH, HD), F32),
            pltpu.VMEM((N, ROWS, HD), BF16),
            pltpu.VMEM((N, ROWS, HD), BF16),
            pltpu.VMEM((N * ROWS, HD), F32),
            pltpu.VMEM((N, ROWS, FB), BF16),
            pltpu.VMEM((N, ROWS, FB), BF16),
            pltpu.VMEM((N, ROWS, FB), BF16),
            pltpu.VMEM((N, ROWS, NB * HB), BF16),
            pltpu.VMEM((N, ROWS, FB), BF16),
            pltpu.VMEM((N, ROWS, FB), BF16),
            pltpu.VMEM((N, ROWS, HD), BF16),
            pltpu.VMEM((N, ROWS, HD), BF16),
            dma((7,)), dma((3,)),
            dma((3, 3)), dma((3, 3)),
            dma((3, 3, 2)), dma((3, 3, 2)),
            dma((2,)), dma((2,)),
            pltpu.SemaphoreType.REGULAR,
            dma((7,)), dma((7,)),
            dma((7,)), dma((7,)),
            dma((8,)), dma((8,)),
            dma((7,)), dma((7,)),
            dma((8,)), dma((8,)),
            dma((7,)), dma((7,)),
        ],
        compiler_params=pltpu.CompilerParams(
            collective_id=0, has_side_effects=True, vmem_limit_bytes=60 * 1024 * 1024
        ),
        cost_estimate=pl.CostEstimate(flops=1_400_000_000, bytes_accessed=5_000_000, transcendentals=100_000),
    )(lengths, q, ck, cv, nk, nv, residual, gain.reshape(QH, HD), gate, up, down)


def solution(mesh):
    rows = ("pair", "role", "shard")
    return jax.shard_map(
        per_device,
        mesh=mesh,
        in_specs=(
            P(rows, None, None), P(rows, None, None), P(rows, None, None), P(rows, None), P(rows, None), P(rows),
            P(rows, None), P(), P("role", "shard"), P("role", "shard"), P("shard", "role"),
        ),
        out_specs=P(rows, None),
        check_vma=False,
    )
```

```python
import jax
import jax.numpy as jnp
from jax import lax
from jax.experimental import pallas as pl
from jax.experimental.pallas import tpu as pltpu
from jax.sharding import PartitionSpec as P

MESH = pl.DeviceIdType.MESH
F32 = jnp.float32
BF16 = jnp.bfloat16
R = 6
HD = 128
QH = 64
KVH = 4
GRP = QH // KVH
L = 128
N = 8
ROWS = R * N
FB = 1024
HB = 128
NB = 4
HALF = FB // 2


def mod(a, n):
    return lax.rem(a + 4 * n, n)


def kernel(
    len_ref, q_hbm, ck_hbm, cv_hbm, nk_hbm, nv_hbm, res_hbm, gain_hbm, gate_hbm, up_hbm, down_hbm,
    out_ref,
    q_ref, ck, cv, nk_ref, nv_ref, res_ref, gain_ref, wgu, wd, scores, mixed, natural, n_send, n_recv, relay,
    acts, terms, rz_send, rz_recv, hid, ry_send, ry_recv, f_send, f_recv,
    local_sem, own_sem, wz_ssem, wz_rsem, wx_ssem, wx_rsem, wc_ssem, wc_rsem, ready_sem, a1_ssem, a1_rsem, ag_ssem, ag_rsem,
    rz_ssem, rz_rsem, hg_ssem, hg_rsem, ry_ssem, ry_rsem, a2_ssem, a2_rsem,
):
    pair, role, shard = lax.axis_index("pair"), lax.axis_index("role"), lax.axis_index("shard")
    x, c = pair // 2, lax.rem(pair, 2)
    z_hi, y = shard // 8, lax.rem(shard, 8)
    z = z_hi * 2 + role

    def at_z(k):
        to = mod(z + k, 8)
        return (pair, lax.rem(to, 2), (to // 2) * 8 + y)

    def at_y(k):
        return (pair, role, z_hi * 8 + mod(y + k, 8))

    def at_x(k):
        return (mod(x + k, 4) * 2 + c, role, shard)

    sibling = (x * 2 + (1 - c), role, shard)

    def remote(src, dst, ssem, rsem, to):
        return pltpu.make_async_remote_copy(
            src_ref=src, dst_ref=dst, send_sem=ssem, recv_sem=rsem, device_id=to, device_id_type=MESH
        )

    operands = []
    for i, (src, dst) in enumerate((
        (q_hbm, q_ref), (ck_hbm, ck), (cv_hbm, cv), (nk_hbm, nk_ref), (nv_hbm, nv_ref), (res_hbm, res_ref), (gain_hbm, gain_ref),
    )):
        copy = pltpu.make_async_copy(src, dst, local_sem.at[i])
        copy.start()
        operands.append(copy)
    quarter = pl.ds(pl.multiple_of(z_hi * FB, FB), FB)
    own = []
    for i, (src, dst) in enumerate((
        (gate_hbm.at[quarter, :], wgu.at[0, :, pl.ds(0, HB)]),
        (up_hbm.at[quarter, :], wgu.at[0, :, pl.ds(HB, HB)]),
        (down_hbm.at[:, quarter], wd.at[0]),
    )):
        copy = pltpu.make_async_copy(src, dst, own_sem.at[i])
        copy.start()
        own.append(copy)

    barrier = pltpu.get_barrier_semaphore()

    def greet(to):
        pl.semaphore_signal(barrier, inc=1, device_id=to, device_id_type=MESH)

    for k in range(1, 8):
        greet(at_z(k))
    for k in (1, 2, 6, 7):
        greet(at_y(k))

    @pl.when(c == 0)
    def _():
        for k in range(1, 4):
            greet(at_x(k))
        greet(sibling)
        pl.semaphore_wait(barrier, 14)

    @pl.when(c == 1)
    def _():
        pl.semaphore_wait(barrier, 12)
        pl.semaphore_signal(ready_sem, inc=1, device_id=sibling, device_id_type=MESH)

    part = pl.ds(pl.multiple_of(x * 256, 256), 256)
    part_d = pl.ds(pl.multiple_of(x * 32, 32), 32)

    def weight_z(k, i):
        q_to = mod(z_hi + k, 4)
        rows = pl.ds(pl.multiple_of(q_to * FB + x * 256, 256), 256)
        cols = pl.ds(pl.multiple_of(q_to * FB, FB), FB)
        src, dst = (
            (gate_hbm.at[rows, :], wgu.at[4 - k, part, pl.ds(0, HB)]),
            (up_hbm.at[rows, :], wgu.at[4 - k, part, pl.ds(HB, HB)]),
            (down_hbm.at[part_d, cols], wd.at[4 - k, part_d, :]),
        )[i]
        return remote(src, dst, wz_ssem.at[k - 1, i], wz_rsem.at[k - 1, i], (pair, role, q_to * 8 + y))

    def weight_x(k, to, i):
        ref = (wgu.at[4 - k, part, :], wd.at[4 - k, part_d, :])[i]
        return remote(ref, ref, wx_ssem.at[k - 1, to - 1, i], wx_rsem.at[k - 1, to - 1, i], at_x(to))

    def weight_c(i):
        ref = (wgu, wd)[i].at[pl.ds(1, 3)]
        return remote(ref, ref, wc_ssem.at[i], wc_rsem.at[i], sibling)

    @pl.when(c == 0)
    def _():
        for k in (1, 3):
            weight_z(k, 0).start()
            weight_z(k, 1).start()

    for copy in operands[:2]:
        copy.wait()
    for r in range(R):
        for k in range(KVH):
            scores[pl.ds(QH * r + GRP * k, GRP), :] = lax.dot_general(
                q_ref[r, pl.ds(GRP * k, GRP), :], ck[r, :, pl.ds(HD * k, HD)],
                (((1,), (1,)), ((), ())), preferred_element_type=F32,
            )
    for copy in operands[2:]:
        copy.wait()
    for i in range(QH):
        mixed[pl.ds(i, R, stride=QH), :] = res_ref[:, pl.ds(HD * i, HD)].astype(F32)
    scale = F32(1.0) / jnp.sqrt(F32(HD))
    slot = lax.broadcasted_iota(jnp.int32, (QH, L), 1)
    for r in range(R):
        rows = pl.ds(QH * r, QH)
        keys = [jnp.broadcast_to(nk_ref[pl.ds(r, 1), pl.ds(HD * k, HD)].astype(F32), (GRP, HD)) for k in range(KVH)]
        vals = [jnp.broadcast_to(nv_ref[pl.ds(r, 1), pl.ds(HD * k, HD)].astype(F32), (GRP, HD)) for k in range(KVH)]
        own_score = jnp.sum(q_ref[r].astype(F32) * jnp.concatenate(keys, 0), axis=1, keepdims=True) * scale
        valid = slot < len_ref[r]
        kept = jnp.where(valid, scores[rows, :] * scale, F32(-1e30))
        top = jnp.maximum(jnp.max(kept, axis=1, keepdims=True), own_score)
        weights = jnp.where(valid, jnp.exp(kept - top), F32(0.0))
        own_weight = jnp.exp(own_score - top)
        total = jnp.sum(weights, axis=1, keepdims=True) + own_weight
        low = weights.astype(BF16)
        summed = jnp.concatenate(
            [
                jnp.dot(low[GRP * k:GRP * (k + 1)], cv[r, :, pl.ds(HD * k, HD)], preferred_element_type=F32)
                for k in range(KVH)
            ], 0,
        )
        summed = summed + own_weight.astype(BF16).astype(F32) * jnp.concatenate(vals, 0)
        mix = mixed[rows, :] + summed / total
        mixed[rows, :] = mix
        mean = jnp.sum(jnp.sum(mix * mix, axis=1, keepdims=True), axis=0, keepdims=True) * F32(1.0 / (QH * HD))
        natural[rows, :] = mix * lax.rsqrt(mean + F32(1e-5)) * gain_ref[...]

    for e in range(N):
        n_send[e] = jnp.concatenate([natural[pl.ds(QH * r + 8 * e, 8), :] for r in range(R)], 0).astype(BF16)

    def tile_of(at):
        return lax.rem(at, 2) * 4 + at // 2

    far_first = (4, 3, 5, 2, 6, 1, 7)
    a1 = [
        remote(n_send.at[tile_of(mod(z + k, 8))], n_recv.at[z], a1_ssem.at[k - 1], a1_rsem.at[k - 1], at_z(k))
        for k in far_first
    ]
    for copy in a1:
        copy.start()
    n_recv[z] = n_send[tile_of(z)]

    @pl.when(c == 0)
    def _():
        weight_z(2, 0).start()
        weight_z(2, 1).start()
        for k in (1, 3):
            weight_z(k, 0).wait_recv()
            weight_z(k, 1).wait_recv()
            for to in (2, 1, 3):
                weight_x(k, to, 0).start()

    for copy in a1:
        copy.wait_recv()
    relay[...] = n_recv[...].reshape(N * ROWS, HD).astype(F32)
    acts[0] = jnp.concatenate([relay[pl.ds(i, ROWS, stride=8), :] for i in range(8)], 1).astype(BF16)

    sent = []

    def push(*args):
        copy = remote(*args)
        copy.start()
        sent.append(copy)
        return copy

    def gather(buf, at, ssem, rsem, width, visit, begun):
        half = width // 2
        cols = [pl.ds(0, half), pl.ds(half, half)]
        two = {}
        for i in range(2):
            for way, k in enumerate((2, 6)):
                s = i if way == 0 else 1 - i
                n = 2 * way + s
                two[way, s] = push(buf.at[0, :, cols[s]], buf.at[k, :, cols[s]], ssem.at[n], rsem.at[n], at(k))
        one = [push(buf.at[0], buf.at[k], ssem.at[4 + n], rsem.at[4 + n], at(k)) for n, k in enumerate((1, 7))]
        begun()
        four, three = [], {}
        for i in range(2):
            for way, k in enumerate((2, 6)):
                s = i if way == 0 else 1 - i
                two[way, s].wait_recv()
                if i == 0:
                    n = 6 + way
                    four.append(push(buf.at[k, :, cols[s]], buf.at[4, :, cols[s]], ssem.at[n], rsem.at[n], at(k)))
                n = 8 + 2 * way + s
                to, place = ((1, 3), (7, 5))[way]
                three[way, s] = push(buf.at[k, :, cols[s]], buf.at[place, :, cols[s]], ssem.at[n], rsem.at[n], at(to))
        visit((0, 2, 6))
        for copy in one:
            copy.wait_recv()
        visit((1, 7))
        for copy in list(three.values()) + four:
            copy.wait_recv()
        visit((3, 5, 4))

    def scatter(term, at, ssem, rsem, sbuf, rbuf):
        cols = [pl.ds(0, HALF), pl.ds(HALF, HALF)]

        def send(value, place, s, n, k):
            sbuf[place, :, cols[s]] = value.astype(BF16)
            ref = sbuf.at[place, :, cols[s]]
            return push(ref, rbuf.at[place, :, cols[s]], ssem.at[n], rsem.at[n], at(k))

        four = [send(term(4, s), 4, s, s, (2, 6)[s]) for s in range(2)]
        three = {}
        for i in range(2):
            for way in range(2):
                s = 1 - i if way == 0 else i
                three[way, s] = send(term((3, 5)[way], s), (3, 5)[way], s, 2 + 2 * way + s, (1, 7)[way])
        one = [send(term(k, s), k, s, 6 + 2 * way + s, k) for way, k in enumerate((1, 7)) for s in range(2)]
        two = []
        for i in range(2):
            for way, k in enumerate((2, 6)):
                s = 1 - i if way == 0 else i
                value = term(k, s)
                three[way, s].wait_recv()
                value = value + rbuf[(3, 5)[way], :, cols[s]].astype(F32)
                if i == 1:
                    four[s].wait_recv()
                    value = value + rbuf[4, :, cols[s]].astype(F32)
                two.append(send(value, k, s, 10 + 2 * way + s, k))
        for copy in one + two:
            copy.wait_recv()
        out = []
        for s in range(2):
            value = term(0, s)
            for k in (1, 7, 2, 6):
                value = value + rbuf[k, :, cols[s]].astype(F32)
            out.append(value)
        return out

    def weights_begun():
        @pl.when(c == 0)
        def _():
            for k in (1, 3, 2):
                weight_z(k, 2).start()
            weight_z(2, 0).wait_recv()
            weight_z(2, 1).wait_recv()
            for to in (2, 1, 3):
                weight_x(2, to, 0).start()

    def gate_up(places):
        if 0 in places:
            own[0].wait()
            own[1].wait()

            @pl.when(c == 0)
            def _():
                for k in (1, 3, 2):
                    weight_z(k, 2).wait_recv()
                    for to in (2, 1, 3):
                        weight_x(k, to, 1).start()
                for k in (1, 3, 2):
                    for to in (2, 1, 3):
                        weight_x(k, to, 0).wait_recv()

            @pl.when(c == 1)
            def _():
                weight_c(0).wait_recv()

        rows = jnp.concatenate([acts[k] for k in places], 0)
        for b in range(NB):
            sums = jnp.dot(rows, wgu[mod(b - z_hi, 4)], preferred_element_type=F32)
            for n, k in enumerate(places):
                terms[k, :, pl.ds(2 * HB * b, 2 * HB)] = sums[ROWS * n:ROWS * (n + 1)]

    gather(acts, at_y, ag_ssem, ag_rsem, FB, gate_up, weights_begun)

    @pl.when(c == 0)
    def _():
        pl.semaphore_wait(ready_sem, 1)
        weight_c(0).start()

    def for_z(k, s):
        return terms[mod(y - z - k, 8), :, pl.ds(s * HALF, HALF)]

    both = scatter(for_z, at_z, rz_ssem, rz_rsem, rz_send, rz_recv)
    for b in range(NB):
        gate = both[b // 2][:, 2 * HB * (b % 2):2 * HB * (b % 2) + HB]
        up = both[b // 2][:, 2 * HB * (b % 2) + HB:2 * HB * (b % 2 + 1)]
        hid[0, :, pl.ds(HB * b, HB)] = (gate / (F32(1.0) + jnp.exp(-gate)) * up).astype(BF16)

    def down(places):
        if 0 in places:
            own[2].wait()

            @pl.when(c == 0)
            def _():
                for k in (1, 3, 2):
                    for to in (2, 1, 3):
                        weight_x(k, to, 1).wait_recv()
                weight_c(1).start()

            @pl.when(c == 1)
            def _():
                weight_c(1).wait_recv()

        rows = jnp.concatenate([hid[k] for k in places], 0)
        total = None
        for b in range(NB):
            term = jnp.dot(rows[:, HB * b:HB * (b + 1)], wd[mod(b - z_hi, 4)], preferred_element_type=F32)
            total = term if total is None else total + term
        for n, k in enumerate(places):
            terms[k] = total[ROWS * n:ROWS * (n + 1)]

    gather(hid, at_z, hg_ssem, hg_rsem, NB * HB, down, lambda: None)

    def for_y(k, s):
        return terms[mod(z - y - k, 8), :, pl.ds(s * HALF, HALF)]

    feed = scatter(for_y, at_y, ry_ssem, ry_rsem, ry_send, ry_recv)
    for i in range(8):
        relay[pl.ds(i, ROWS, stride=8), :] = feed[i // 4][:, HD * (i % 4):HD * (i % 4 + 1)]
    f_send[...] = relay[...].astype(BF16).reshape(N, ROWS, HD)

    me = tile_of(z)
    a2 = [
        remote(f_send.at[mod(z + k, 8)], f_recv.at[me], a2_ssem.at[k - 1], a2_rsem.at[k - 1], at_z(k)) for k in far_first
    ]
    for copy in a2:
        copy.start()
    f_recv[me] = f_send[z]
    for copy in a2:
        copy.wait_recv()
    for e in range(N):
        mix = jnp.concatenate([mixed[pl.ds(QH * r + 8 * e, 8), :] for r in range(R)], 0)
        natural[pl.ds(ROWS * e, ROWS), :] = mix + f_recv[e].astype(F32)
    for e in range(N):
        for i in range(8):
            out_ref[:, pl.ds(FB * e + HD * i, HD)] = natural[pl.ds(ROWS * e + i, R, stride=8), :].astype(BF16)

    for copy in a1 + a2 + sent:
        copy.wait_send()

    @pl.when(c == 0)
    def _():
        for k in (1, 2, 3):
            for i in range(3):
                weight_z(k, i).wait_send()
            for to in (1, 2, 3):
                for i in range(2):
                    weight_x(k, to, i).wait_send()
        for i in range(2):
            weight_c(i).wait_send()


def per_device(q, ck, cv, nk, nv, lengths, residual, gain, gate, up, down):
    vmem = pl.BlockSpec(memory_space=pltpu.VMEM)
    smem = pl.BlockSpec(memory_space=pltpu.SMEM)
    hbm = pl.BlockSpec(memory_space=pl.ANY)
    dma = pltpu.SemaphoreType.DMA
    return pl.pallas_call(
        kernel,
        out_shape=jax.ShapeDtypeStruct((R, QH * HD), BF16),
        in_specs=[smem] + [hbm] * 10,
        out_specs=vmem,
        scratch_shapes=[
            pltpu.VMEM((R, QH, HD), BF16),
            pltpu.VMEM((R, L, KVH * HD), BF16),
            pltpu.VMEM((R, L, KVH * HD), BF16),
            pltpu.VMEM((R, KVH * HD), BF16),
            pltpu.VMEM((R, KVH * HD), BF16),
            pltpu.VMEM((R, QH * HD), BF16),
            pltpu.VMEM((QH, HD), F32),
            pltpu.VMEM((NB, FB, 2 * HB), BF16),
            pltpu.VMEM((NB, HB, FB), BF16),
            pltpu.VMEM((R * QH, L), F32),
            pltpu.VMEM((R * QH, HD), F32),
            pltpu.VMEM((R * QH, HD), F32),
            pltpu.VMEM((N, ROWS, HD), BF16),
            pltpu.VMEM((N, ROWS, HD), BF16),
            pltpu.VMEM((N * ROWS, HD), F32),
            pltpu.VMEM((N, ROWS, FB), BF16),
            pltpu.VMEM((N, ROWS, FB), F32),
            pltpu.VMEM((N, ROWS, FB), BF16),
            pltpu.VMEM((N, ROWS, FB), BF16),
            pltpu.VMEM((N, ROWS, NB * HB), BF16),
            pltpu.VMEM((N, ROWS, FB), BF16),
            pltpu.VMEM((N, ROWS, FB), BF16),
            pltpu.VMEM((N, ROWS, HD), BF16),
            pltpu.VMEM((N, ROWS, HD), BF16),
            dma((7,)), dma((3,)),
            dma((3, 3)), dma((3, 3)),
            dma((3, 3, 2)), dma((3, 3, 2)),
            dma((2,)), dma((2,)),
            pltpu.SemaphoreType.REGULAR,
            dma((7,)), dma((7,)),
            dma((12,)), dma((12,)),
            dma((14,)), dma((14,)),
            dma((12,)), dma((12,)),
            dma((14,)), dma((14,)),
            dma((7,)), dma((7,)),
        ],
        compiler_params=pltpu.CompilerParams(
            collective_id=0, has_side_effects=True, vmem_limit_bytes=60 * 1024 * 1024
        ),
        cost_estimate=pl.CostEstimate(flops=1_400_000_000, bytes_accessed=5_000_000, transcendentals=100_000),
    )(lengths, q, ck, cv, nk, nv, residual, gain.reshape(QH, HD), gate, up, down)


def solution(mesh):
    rows = ("pair", "role", "shard")
    return jax.shard_map(
        per_device,
        mesh=mesh,
        in_specs=(
            P(rows, None, None), P(rows, None, None), P(rows, None, None), P(rows, None), P(rows, None), P(rows),
            P(rows, None), P(), P("role", "shard"), P("role", "shard"), P("shard", "role"),
        ),
        out_specs=P(rows, None),
        check_vma=False,
    )
```

```python
import jax
import jax.numpy as jnp
from jax import lax
from jax.experimental import pallas as pl
from jax.experimental.pallas import tpu as pltpu
from jax.sharding import PartitionSpec as P

MESH = pl.DeviceIdType.MESH
F32 = jnp.float32
BF16 = jnp.bfloat16
R = 6
HD = 128
QH = 64
KVH = 4
GRP = QH // KVH
L = 128
N = 8
ROWS = R * N
FB = 1024
HB = 128
NB = 4
HALF = FB // 2


def mod(a, n):
    return lax.rem(a + 4 * n, n)


def kernel(
    len_hbm, q_hbm, ck_hbm, cv_hbm, nk_hbm, nv_hbm, res_hbm, gain_hbm, gate_hbm, up_hbm, down_hbm,
    out_ref,
    len_ref, q_ref, ck, cv, nk_ref, nv_ref, res_ref, gain_ref, wgu, wd, scores, mixed, natural, n_send, n_recv, relay,
    acts, terms, rz_send, rz_recv, hid, ry_send, ry_recv, f_send, f_recv,
    local_sem, own_sem, wz_ssem, wz_rsem, wx_ssem, wx_rsem, wc_ssem, wc_rsem, a1_ssem, a1_rsem, ag_ssem, ag_rsem,
    rz_ssem, rz_rsem, hg_ssem, hg_rsem, ry_ssem, ry_rsem, a2_ssem, a2_rsem,
):
    pair, role, shard = lax.axis_index("pair"), lax.axis_index("role"), lax.axis_index("shard")
    x, c = pair // 2, lax.rem(pair, 2)
    z_hi, y = shard // 8, lax.rem(shard, 8)
    z = z_hi * 2 + role

    def at_z(k):
        to = mod(z + k, 8)
        return (pair, lax.rem(to, 2), (to // 2) * 8 + y)

    def at_y(k):
        return (pair, role, z_hi * 8 + mod(y + k, 8))

    def at_x(k):
        return (mod(x + k, 4) * 2 + c, role, shard)

    sibling = (x * 2 + (1 - c), role, shard)

    def remote(src, dst, ssem, rsem, to):
        return pltpu.make_async_remote_copy(
            src_ref=src, dst_ref=dst, send_sem=ssem, recv_sem=rsem, device_id=to, device_id_type=MESH
        )

    operands = []
    for i, (src, dst) in enumerate((
        (q_hbm, q_ref), (ck_hbm, ck), (len_hbm, len_ref), (cv_hbm, cv), (nk_hbm, nk_ref), (nv_hbm, nv_ref), (res_hbm, res_ref), (gain_hbm, gain_ref),
    )):
        copy = pltpu.make_async_copy(src, dst, local_sem.at[i])
        copy.start()
        operands.append(copy)
    quarter = pl.ds(pl.multiple_of(z_hi * FB, FB), FB)
    own = []
    for i, (src, dst) in enumerate((
        (gate_hbm.at[quarter, :], wgu.at[0, :, pl.ds(0, HB)]),
        (up_hbm.at[quarter, :], wgu.at[0, :, pl.ds(HB, HB)]),
        (down_hbm.at[:, quarter], wd.at[0]),
    )):
        copy = pltpu.make_async_copy(src, dst, own_sem.at[i])
        copy.start()
        own.append(copy)

    barrier = pltpu.get_barrier_semaphore()

    def greet(to):
        pl.semaphore_signal(barrier, inc=1, device_id=to, device_id_type=MESH)

    for k in range(1, 8):
        greet(at_z(k))
    for k in (1, 2, 6, 7):
        greet(at_y(k))

    for k in range(1, 4):
        greet(at_x(k))
    greet(sibling)
    pl.semaphore_wait(barrier, 15)

    p = c * 4 + x
    part = pl.ds(pl.multiple_of(p * 128, 128), 128)
    part_d = pl.ds(pl.multiple_of(p * 16, 16), 16)

    def weight_z(k, i):
        q_to = mod(z_hi + k, 4)
        rows = pl.ds(pl.multiple_of(q_to * FB + p * 128, 128), 128)
        cols = pl.ds(pl.multiple_of(q_to * FB, FB), FB)
        src, dst = (
            (gate_hbm.at[rows, :], wgu.at[4 - k, part, pl.ds(0, HB)]),
            (up_hbm.at[rows, :], wgu.at[4 - k, part, pl.ds(HB, HB)]),
            (down_hbm.at[part_d, cols], wd.at[4 - k, part_d, :]),
        )[i]
        return remote(src, dst, wz_ssem.at[k - 1, i], wz_rsem.at[k - 1, i], (pair, role, q_to * 8 + y))

    def weight_x(k, to, i):
        ref = (wgu.at[4 - k, part, :], wd.at[4 - k, part_d, :])[i]
        return remote(ref, ref, wx_ssem.at[k - 1, to - 1, i], wx_rsem.at[k - 1, to - 1, i], at_x(to))

    for k in (1, 3):
        weight_z(k, 0).start()
        weight_z(k, 1).start()

    def weight_c(k, i):
        ref = (
            wgu.at[4 - k, pl.ds(pl.multiple_of(c * 512, 512), 512), :],
            wd.at[4 - k, pl.ds(pl.multiple_of(c * 64, 64), 64), :],
        )[i]
        return remote(ref, ref, wc_ssem.at[k - 1, i], wc_rsem.at[k - 1, i], sibling)

    for copy in operands[:2]:
        copy.wait()
    for r in range(R):
        for k in range(KVH):
            scores[pl.ds(QH * r + GRP * k, GRP), :] = lax.dot_general(
                q_ref[r, pl.ds(GRP * k, GRP), :], ck[r, :, pl.ds(HD * k, HD)],
                (((1,), (1,)), ((), ())), preferred_element_type=F32,
            )
    for copy in operands[2:]:
        copy.wait()
    for i in range(QH):
        mixed[pl.ds(i, R, stride=QH), :] = res_ref[:, pl.ds(HD * i, HD)].astype(F32)
    scale = F32(1.0) / jnp.sqrt(F32(HD))
    slot = lax.broadcasted_iota(jnp.int32, (QH, L), 1)
    for r in range(R):
        rows = pl.ds(QH * r, QH)
        keys = [jnp.broadcast_to(nk_ref[pl.ds(r, 1), pl.ds(HD * k, HD)].astype(F32), (GRP, HD)) for k in range(KVH)]
        vals = [jnp.broadcast_to(nv_ref[pl.ds(r, 1), pl.ds(HD * k, HD)].astype(F32), (GRP, HD)) for k in range(KVH)]
        own_score = jnp.sum(q_ref[r].astype(F32) * jnp.concatenate(keys, 0), axis=1, keepdims=True) * scale
        valid = slot < len_ref[r]
        kept = jnp.where(valid, scores[rows, :] * scale, F32(-1e30))
        top = jnp.maximum(jnp.max(kept, axis=1, keepdims=True), own_score)
        weights = jnp.where(valid, jnp.exp(kept - top), F32(0.0))
        own_weight = jnp.exp(own_score - top)
        total = jnp.sum(weights, axis=1, keepdims=True) + own_weight
        low = weights.astype(BF16)
        summed = jnp.concatenate(
            [
                jnp.dot(low[GRP * k:GRP * (k + 1)], cv[r, :, pl.ds(HD * k, HD)], preferred_element_type=F32)
                for k in range(KVH)
            ], 0,
        )
        summed = summed + own_weight.astype(BF16).astype(F32) * jnp.concatenate(vals, 0)
        mix = mixed[rows, :] + summed / total
        mixed[rows, :] = mix
        mean = jnp.sum(jnp.sum(mix * mix, axis=1, keepdims=True), axis=0, keepdims=True) * F32(1.0 / (QH * HD))
        natural[rows, :] = mix * lax.rsqrt(mean + F32(1e-5)) * gain_ref[...]

    for e in range(N):
        n_send[e] = jnp.concatenate([natural[pl.ds(QH * r + 8 * e, 8), :] for r in range(R)], 0).astype(BF16)

    def tile_of(at):
        return lax.rem(at, 2) * 4 + at // 2

    far_first = (4, 3, 5, 2, 6, 1, 7)
    a1 = [
        remote(n_send.at[tile_of(mod(z + k, 8))], n_recv.at[z], a1_ssem.at[k - 1], a1_rsem.at[k - 1], at_z(k))
        for k in far_first
    ]
    for copy in a1:
        copy.start()
    n_recv[z] = n_send[tile_of(z)]

    weight_z(2, 0).start()
    weight_z(2, 1).start()
    for k in (1, 3):
        weight_z(k, 0).wait_recv()
        weight_z(k, 1).wait_recv()
        for to in (2, 1, 3):
            weight_x(k, to, 0).start()

    for copy in a1:
        copy.wait_recv()
    relay[...] = n_recv[...].reshape(N * ROWS, HD).astype(F32)
    acts[0] = jnp.concatenate([relay[pl.ds(i, ROWS, stride=8), :] for i in range(8)], 1).astype(BF16)

    sent = []

    def push(*args):
        copy = remote(*args)
        copy.start()
        sent.append(copy)
        return copy

    def gather(buf, at, ssem, rsem, width, visit, begun):
        half = width // 2
        cols = [pl.ds(0, half), pl.ds(half, half)]
        two = {}
        for i in range(2):
            for way, k in enumerate((2, 6)):
                s = i if way == 0 else 1 - i
                n = 2 * way + s
                two[way, s] = push(buf.at[0, :, cols[s]], buf.at[k, :, cols[s]], ssem.at[n], rsem.at[n], at(k))
        one = [push(buf.at[0], buf.at[k], ssem.at[4 + n], rsem.at[4 + n], at(k)) for n, k in enumerate((1, 7))]
        begun()
        four, three = [], {}
        for i in range(2):
            for way, k in enumerate((2, 6)):
                s = i if way == 0 else 1 - i
                two[way, s].wait_recv()
                if i == 0:
                    n = 6 + way
                    four.append(push(buf.at[k, :, cols[s]], buf.at[4, :, cols[s]], ssem.at[n], rsem.at[n], at(k)))
                n = 8 + 2 * way + s
                to, place = ((1, 3), (7, 5))[way]
                three[way, s] = push(buf.at[k, :, cols[s]], buf.at[place, :, cols[s]], ssem.at[n], rsem.at[n], at(to))
        visit((0, 2, 6))
        for copy in one:
            copy.wait_recv()
        visit((1, 7))
        for copy in list(three.values()) + four:
            copy.wait_recv()
        visit((3, 5, 4))

    def scatter(term, at, ssem, rsem, sbuf, rbuf):
        cols = [pl.ds(0, HALF), pl.ds(HALF, HALF)]

        def send(value, place, s, n, k):
            sbuf[place, :, cols[s]] = value.astype(BF16)
            ref = sbuf.at[place, :, cols[s]]
            return push(ref, rbuf.at[place, :, cols[s]], ssem.at[n], rsem.at[n], at(k))

        four = [send(term(4, s), 4, s, s, (2, 6)[s]) for s in range(2)]
        three = {}
        for i in range(2):
            for way in range(2):
                s = 1 - i if way == 0 else i
                three[way, s] = send(term((3, 5)[way], s), (3, 5)[way], s, 2 + 2 * way + s, (1, 7)[way])
        one = [send(term(k, s), k, s, 6 + 2 * way + s, k) for way, k in enumerate((1, 7)) for s in range(2)]
        two = []
        for i in range(2):
            for way, k in enumerate((2, 6)):
                s = 1 - i if way == 0 else i
                value = term(k, s)
                three[way, s].wait_recv()
                value = value + rbuf[(3, 5)[way], :, cols[s]].astype(F32)
                if i == 1:
                    four[s].wait_recv()
                    value = value + rbuf[4, :, cols[s]].astype(F32)
                two.append(send(value, k, s, 10 + 2 * way + s, k))
        for copy in one + two:
            copy.wait_recv()
        out = []
        for s in range(2):
            value = term(0, s)
            for k in (1, 7, 2, 6):
                value = value + rbuf[k, :, cols[s]].astype(F32)
            out.append(value)
        return out

    def weights_begun():
        for k in (1, 3, 2):
            weight_z(k, 2).start()
        weight_z(2, 0).wait_recv()
        weight_z(2, 1).wait_recv()
        for to in (2, 1, 3):
            weight_x(2, to, 0).start()

    def gate_up(places):
        if 0 in places:
            own[0].wait()
            own[1].wait()

            for k in (1, 3, 2):
                for to in (1, 3, 2):
                    weight_x(k, to, 0).wait_recv()
                weight_c(k, 0).start()
            for k in (1, 3, 2):
                weight_z(k, 2).wait_recv()
                for to in (2, 1, 3):
                    weight_x(k, to, 1).start()
            for k in (1, 3, 2):
                weight_c(k, 0).wait_recv()

        rows = jnp.concatenate([acts[k] for k in places], 0)
        for b in range(NB):
            sums = jnp.dot(rows, wgu[mod(b - z_hi, 4)], preferred_element_type=F32)
            for n, k in enumerate(places):
                terms[k, :, pl.ds(2 * HB * b, 2 * HB)] = sums[ROWS * n:ROWS * (n + 1)]

    gather(acts, at_y, ag_ssem, ag_rsem, FB, gate_up, weights_begun)

    def for_z(k, s):
        return terms[mod(y - z - k, 8), :, pl.ds(s * HALF, HALF)]

    both = scatter(for_z, at_z, rz_ssem, rz_rsem, rz_send, rz_recv)
    for b in range(NB):
        gate = both[b // 2][:, 2 * HB * (b % 2):2 * HB * (b % 2) + HB]
        up = both[b // 2][:, 2 * HB * (b % 2) + HB:2 * HB * (b % 2 + 1)]
        hid[0, :, pl.ds(HB * b, HB)] = (gate / (F32(1.0) + jnp.exp(-gate)) * up).astype(BF16)

    def down(places):
        if 0 in places:
            own[2].wait()

            for k in (1, 3, 2):
                weight_c(k, 1).wait_recv()

        rows = jnp.concatenate([hid[k] for k in places], 0)
        total = None
        for b in range(NB):
            term = jnp.dot(rows[:, HB * b:HB * (b + 1)], wd[mod(b - z_hi, 4)], preferred_element_type=F32)
            total = term if total is None else total + term
        for n, k in enumerate(places):
            terms[k] = total[ROWS * n:ROWS * (n + 1)]

    def hand_down():
        for k in (1, 3, 2):
            for to in (1, 3, 2):
                weight_x(k, to, 1).wait_recv()
            weight_c(k, 1).start()

    gather(hid, at_z, hg_ssem, hg_rsem, NB * HB, down, hand_down)

    def for_y(k, s):
        return terms[mod(z - y - k, 8), :, pl.ds(s * HALF, HALF)]

    feed = scatter(for_y, at_y, ry_ssem, ry_rsem, ry_send, ry_recv)
    for i in range(8):
        relay[pl.ds(i, ROWS, stride=8), :] = feed[i // 4][:, HD * (i % 4):HD * (i % 4 + 1)]
    f_send[...] = relay[...].astype(BF16).reshape(N, ROWS, HD)

    me = tile_of(z)
    a2 = [
        remote(f_send.at[mod(z + k, 8)], f_recv.at[me], a2_ssem.at[k - 1], a2_rsem.at[k - 1], at_z(k)) for k in far_first
    ]
    for copy in a2:
        copy.start()
    f_recv[me] = f_send[z]
    for copy in a2:
        copy.wait_recv()
    for e in range(N):
        mix = jnp.concatenate([mixed[pl.ds(QH * r + 8 * e, 8), :] for r in range(R)], 0)
        natural[pl.ds(ROWS * e, ROWS), :] = mix + f_recv[e].astype(F32)
    for e in range(N):
        for i in range(8):
            out_ref[:, pl.ds(FB * e + HD * i, HD)] = natural[pl.ds(ROWS * e + i, R, stride=8), :].astype(BF16)

    for copy in a1 + a2 + sent:
        copy.wait_send()

    for k in (1, 2, 3):
        for i in range(3):
            weight_z(k, i).wait_send()
        for to in (1, 2, 3):
            for i in range(2):
                weight_x(k, to, i).wait_send()
        for i in range(2):
            weight_c(k, i).wait_send()


def per_device(q, ck, cv, nk, nv, lengths, residual, gain, gate, up, down):
    vmem = pl.BlockSpec(memory_space=pltpu.VMEM)
    hbm = pl.BlockSpec(memory_space=pl.ANY)
    dma = pltpu.SemaphoreType.DMA
    return pl.pallas_call(
        kernel,
        out_shape=jax.ShapeDtypeStruct((R, QH * HD), BF16),
        in_specs=[hbm] * 11,
        out_specs=vmem,
        scratch_shapes=[
            pltpu.SMEM((R,), jnp.int32),
            pltpu.VMEM((R, QH, HD), BF16),
            pltpu.VMEM((R, L, KVH * HD), BF16),
            pltpu.VMEM((R, L, KVH * HD), BF16),
            pltpu.VMEM((R, KVH * HD), BF16),
            pltpu.VMEM((R, KVH * HD), BF16),
            pltpu.VMEM((R, QH * HD), BF16),
            pltpu.VMEM((QH, HD), F32),
            pltpu.VMEM((NB, FB, 2 * HB), BF16),
            pltpu.VMEM((NB, HB, FB), BF16),
            pltpu.VMEM((R * QH, L), F32),
            pltpu.VMEM((R * QH, HD), F32),
            pltpu.VMEM((R * QH, HD), F32),
            pltpu.VMEM((N, ROWS, HD), BF16),
            pltpu.VMEM((N, ROWS, HD), BF16),
            pltpu.VMEM((N * ROWS, HD), F32),
            pltpu.VMEM((N, ROWS, FB), BF16),
            pltpu.VMEM((N, ROWS, FB), F32),
            pltpu.VMEM((N, ROWS, FB), BF16),
            pltpu.VMEM((N, ROWS, FB), BF16),
            pltpu.VMEM((N, ROWS, NB * HB), BF16),
            pltpu.VMEM((N, ROWS, FB), BF16),
            pltpu.VMEM((N, ROWS, FB), BF16),
            pltpu.VMEM((N, ROWS, HD), BF16),
            pltpu.VMEM((N, ROWS, HD), BF16),
            dma((8,)), dma((3,)),
            dma((3, 3)), dma((3, 3)),
            dma((3, 3, 2)), dma((3, 3, 2)),
            dma((3, 2)), dma((3, 2)),
            dma((7,)), dma((7,)),
            dma((12,)), dma((12,)),
            dma((14,)), dma((14,)),
            dma((12,)), dma((12,)),
            dma((14,)), dma((14,)),
            dma((7,)), dma((7,)),
        ],
        compiler_params=pltpu.CompilerParams(
            collective_id=0, has_side_effects=True, vmem_limit_bytes=60 * 1024 * 1024
        ),
        cost_estimate=pl.CostEstimate(flops=1_400_000_000, bytes_accessed=5_000_000, transcendentals=100_000),
    )(lengths, q, ck, cv, nk, nv, residual, gain.reshape(QH, HD), gate, up, down)


def solution(mesh):
    rows = ("pair", "role", "shard")
    return jax.shard_map(
        per_device,
        mesh=mesh,
        in_specs=(
            P(rows, None, None), P(rows, None, None), P(rows, None, None), P(rows, None), P(rows, None), P(rows),
            P(rows, None), P(), P("role", "shard"), P("role", "shard"), P("shard", "role"),
        ),
        out_specs=P(rows, None),
        check_vma=False,
    )
```

```python
import jax
import jax.numpy as jnp
from jax import lax
from jax.experimental import pallas as pl
from jax.experimental.pallas import tpu as pltpu
from jax.sharding import PartitionSpec as P

MESH = pl.DeviceIdType.MESH
F32 = jnp.float32
BF16 = jnp.bfloat16
R = 6
HD = 128
QH = 64
KVH = 4
GRP = QH // KVH
L = 128
N = 8
ROWS = R * N
FB = 1024
HB = 128
NB = 4
HALF = FB // 2


def mod(a, n):
    return lax.rem(a + 4 * n, n)


def kernel(
    len_hbm, q_hbm, ck_hbm, cv_hbm, nk_hbm, nv_hbm, res_hbm, gain_hbm, gate_hbm, up_hbm, down_hbm,
    out_ref,
    len_ref, q_ref, ck, cv, nk_ref, nv_ref, res_ref, gain_ref, wgu, wd, scores, mixed, natural, n_send, n_recv, relay,
    acts, terms, rz_send, rz_recv, hid, ry_send, ry_recv, f_send, f_recv,
    local_sem, own_sem, wz_ssem, wz_rsem, wx_ssem, wx_rsem, wc_ssem, wc_rsem, a1_ssem, a1_rsem, ag_ssem, ag_rsem,
    rz_ssem, rz_rsem, hg_ssem, hg_rsem, ry_ssem, ry_rsem, a2_ssem, a2_rsem,
):
    pair, role, shard = lax.axis_index("pair"), lax.axis_index("role"), lax.axis_index("shard")
    x, c = pair // 2, lax.rem(pair, 2)
    z_hi, y = shard // 8, lax.rem(shard, 8)
    z = z_hi * 2 + role

    def at_z(k):
        to = mod(z + k, 8)
        return (pair, lax.rem(to, 2), (to // 2) * 8 + y)

    def at_y(k):
        return (pair, role, z_hi * 8 + mod(y + k, 8))

    def at_x(k):
        return (mod(x + k, 4) * 2 + c, role, shard)

    sibling = (x * 2 + (1 - c), role, shard)

    def remote(src, dst, ssem, rsem, to):
        return pltpu.make_async_remote_copy(
            src_ref=src, dst_ref=dst, send_sem=ssem, recv_sem=rsem, device_id=to, device_id_type=MESH
        )

    operands = []
    for i, (src, dst) in enumerate((
        (q_hbm, q_ref), (ck_hbm, ck), (len_hbm, len_ref), (cv_hbm, cv), (nk_hbm, nk_ref), (nv_hbm, nv_ref), (res_hbm, res_ref), (gain_hbm, gain_ref),
    )):
        copy = pltpu.make_async_copy(src, dst, local_sem.at[i])
        copy.start()
        operands.append(copy)
    quarter = pl.ds(pl.multiple_of(z_hi * FB, FB), FB)
    own = []
    for i, (src, dst) in enumerate((
        (gate_hbm.at[quarter, :], wgu.at[0, :, pl.ds(0, HB)]),
        (up_hbm.at[quarter, :], wgu.at[0, :, pl.ds(HB, HB)]),
        (down_hbm.at[:, quarter], wd.at[0]),
    )):
        copy = pltpu.make_async_copy(src, dst, own_sem.at[i])
        copy.start()
        own.append(copy)

    barrier = pltpu.get_barrier_semaphore()

    def greet(to):
        pl.semaphore_signal(barrier, inc=1, device_id=to, device_id_type=MESH)

    for k in range(1, 8):
        greet(at_z(k))
    for k in (1, 2, 6, 7):
        greet(at_y(k))

    for k in range(1, 4):
        greet(at_x(k))
    greet(sibling)
    pl.semaphore_wait(barrier, 15)

    p = c * 4 + x
    part = pl.ds(pl.multiple_of(p * 128, 128), 128)
    part_d = pl.ds(pl.multiple_of(x * 32, 32), 32)

    def weight_z(k, i):
        q_to = mod(z_hi + k, 4)
        rows = pl.ds(pl.multiple_of(q_to * FB + p * 128, 128), 128)
        cols = pl.ds(pl.multiple_of(q_to * FB, FB), FB)
        src, dst = (
            (gate_hbm.at[rows, :], wgu.at[4 - k, part, pl.ds(0, HB)]),
            (up_hbm.at[rows, :], wgu.at[4 - k, part, pl.ds(HB, HB)]),
            (down_hbm.at[part_d, cols], wd.at[4 - k, part_d, :]),
        )[i]
        return remote(src, dst, wz_ssem.at[k - 1, i], wz_rsem.at[k - 1, i], (pair, role, q_to * 8 + y))

    def weight_x(k, to, i):
        ref = (wgu.at[4 - k, part, :], wd.at[4 - k, part_d, :])[i]
        return remote(ref, ref, wx_ssem.at[k - 1, to - 1, i], wx_rsem.at[k - 1, to - 1, i], at_x(to))

    for k in (1, 3):
        weight_z(k, 0).start()
        weight_z(k, 1).start()

    def weight_c(k, i):
        ref = (
            wgu.at[4 - k, pl.ds(pl.multiple_of(c * 512, 512), 512), :],
            wd.at[4 - k],
        )[i]
        return remote(ref, ref, wc_ssem.at[k - 1, i], wc_rsem.at[k - 1, i], sibling)

    for copy in operands[:2]:
        copy.wait()
    for r in range(R):
        for k in range(KVH):
            scores[pl.ds(QH * r + GRP * k, GRP), :] = lax.dot_general(
                q_ref[r, pl.ds(GRP * k, GRP), :], ck[r, :, pl.ds(HD * k, HD)],
                (((1,), (1,)), ((), ())), preferred_element_type=F32,
            )
    for copy in operands[2:]:
        copy.wait()
    for i in range(QH):
        mixed[pl.ds(i, R, stride=QH), :] = res_ref[:, pl.ds(HD * i, HD)].astype(F32)
    scale = F32(1.0) / jnp.sqrt(F32(HD))
    slot = lax.broadcasted_iota(jnp.int32, (QH, L), 1)
    for r in range(R):
        rows = pl.ds(QH * r, QH)
        keys = [jnp.broadcast_to(nk_ref[pl.ds(r, 1), pl.ds(HD * k, HD)].astype(F32), (GRP, HD)) for k in range(KVH)]
        vals = [jnp.broadcast_to(nv_ref[pl.ds(r, 1), pl.ds(HD * k, HD)].astype(F32), (GRP, HD)) for k in range(KVH)]
        own_score = jnp.sum(q_ref[r].astype(F32) * jnp.concatenate(keys, 0), axis=1, keepdims=True) * scale
        valid = slot < len_ref[r]
        kept = jnp.where(valid, scores[rows, :] * scale, F32(-1e30))
        top = jnp.maximum(jnp.max(kept, axis=1, keepdims=True), own_score)
        weights = jnp.where(valid, jnp.exp(kept - top), F32(0.0))
        own_weight = jnp.exp(own_score - top)
        total = jnp.sum(weights, axis=1, keepdims=True) + own_weight
        low = weights.astype(BF16)
        summed = jnp.concatenate(
            [
                jnp.dot(low[GRP * k:GRP * (k + 1)], cv[r, :, pl.ds(HD * k, HD)], preferred_element_type=F32)
                for k in range(KVH)
            ], 0,
        )
        summed = summed + own_weight.astype(BF16).astype(F32) * jnp.concatenate(vals, 0)
        mix = mixed[rows, :] + summed / total
        mixed[rows, :] = mix
        mean = jnp.sum(jnp.sum(mix * mix, axis=1, keepdims=True), axis=0, keepdims=True) * F32(1.0 / (QH * HD))
        natural[rows, :] = mix * lax.rsqrt(mean + F32(1e-5)) * gain_ref[...]

    for e in range(N):
        n_send[e] = jnp.concatenate([natural[pl.ds(QH * r + 8 * e, 8), :] for r in range(R)], 0).astype(BF16)

    def tile_of(at):
        return lax.rem(at, 2) * 4 + at // 2

    far_first = (4, 3, 5, 2, 6, 1, 7)
    a1 = [
        remote(n_send.at[tile_of(mod(z + k, 8))], n_recv.at[z], a1_ssem.at[k - 1], a1_rsem.at[k - 1], at_z(k))
        for k in far_first
    ]
    for copy in a1:
        copy.start()
    n_recv[z] = n_send[tile_of(z)]

    weight_z(2, 0).start()
    weight_z(2, 1).start()
    for k in (1, 3):
        weight_z(k, 0).wait_recv()
        weight_z(k, 1).wait_recv()
        for to in (2, 1, 3):
            weight_x(k, to, 0).start()

    for copy in a1:
        copy.wait_recv()
    relay[...] = n_recv[...].reshape(N * ROWS, HD).astype(F32)
    acts[0] = jnp.concatenate([relay[pl.ds(i, ROWS, stride=8), :] for i in range(8)], 1).astype(BF16)

    sent = []

    def push(*args):
        copy = remote(*args)
        copy.start()
        sent.append(copy)
        return copy

    def gather(buf, at, ssem, rsem, width, visit, begun):
        half = width // 2
        cols = [pl.ds(0, half), pl.ds(half, half)]
        two = {}
        for i in range(2):
            for way, k in enumerate((2, 6)):
                s = i if way == 0 else 1 - i
                n = 2 * way + s
                two[way, s] = push(buf.at[0, :, cols[s]], buf.at[k, :, cols[s]], ssem.at[n], rsem.at[n], at(k))
        one = [push(buf.at[0], buf.at[k], ssem.at[4 + n], rsem.at[4 + n], at(k)) for n, k in enumerate((1, 7))]
        begun()
        four, three = [], {}
        for i in range(2):
            for way, k in enumerate((2, 6)):
                s = i if way == 0 else 1 - i
                two[way, s].wait_recv()
                if i == 0:
                    n = 6 + way
                    four.append(push(buf.at[k, :, cols[s]], buf.at[4, :, cols[s]], ssem.at[n], rsem.at[n], at(k)))
                n = 8 + 2 * way + s
                to, place = ((1, 3), (7, 5))[way]
                three[way, s] = push(buf.at[k, :, cols[s]], buf.at[place, :, cols[s]], ssem.at[n], rsem.at[n], at(to))
        visit((0, 2, 6))
        for copy in one:
            copy.wait_recv()
        visit((1, 7))
        for copy in list(three.values()) + four:
            copy.wait_recv()
        visit((3, 5, 4))

    def scatter(term, at, ssem, rsem, sbuf, rbuf):
        cols = [pl.ds(0, HALF), pl.ds(HALF, HALF)]

        def send(value, place, s, n, k):
            sbuf[place, :, cols[s]] = value.astype(BF16)
            ref = sbuf.at[place, :, cols[s]]
            return push(ref, rbuf.at[place, :, cols[s]], ssem.at[n], rsem.at[n], at(k))

        four = [send(term(4, s), 4, s, s, (2, 6)[s]) for s in range(2)]
        three = {}
        for i in range(2):
            for way in range(2):
                s = 1 - i if way == 0 else i
                three[way, s] = send(term((3, 5)[way], s), (3, 5)[way], s, 2 + 2 * way + s, (1, 7)[way])
        one = [send(term(k, s), k, s, 6 + 2 * way + s, k) for way, k in enumerate((1, 7)) for s in range(2)]
        two = []
        for i in range(2):
            for way, k in enumerate((2, 6)):
                s = 1 - i if way == 0 else i
                value = term(k, s)
                three[way, s].wait_recv()
                value = value + rbuf[(3, 5)[way], :, cols[s]].astype(F32)
                if i == 1:
                    four[s].wait_recv()
                    value = value + rbuf[4, :, cols[s]].astype(F32)
                two.append(send(value, k, s, 10 + 2 * way + s, k))
        for copy in one + two:
            copy.wait_recv()
        out = []
        for s in range(2):
            value = term(0, s)
            for k in (1, 7, 2, 6):
                value = value + rbuf[k, :, cols[s]].astype(F32)
            out.append(value)
        return out

    def down_along():
        @pl.when(c == 1)
        def _():
            for k in (1, 3, 2):
                weight_z(k, 2).wait_recv()
                for to in (2, 1, 3):
                    weight_x(k, to, 1).start()

    def weights_begun():
        @pl.when(c == 1)
        def _():
            for k in (1, 3, 2):
                weight_z(k, 2).start()

        weight_z(2, 0).wait_recv()
        weight_z(2, 1).wait_recv()
        for to in (2, 1, 3):
            weight_x(2, to, 0).start()

    def gate_up(places):
        if 0 in places:
            own[0].wait()
            own[1].wait()

            for k in (1, 3, 2):
                for to in (1, 3, 2):
                    weight_x(k, to, 0).wait_recv()
                weight_c(k, 0).start()

        rows = jnp.concatenate([acts[k] for k in places], 0)
        for place in (0, 3, 1, 2):
            if 0 in places and place:
                weight_c(4 - place, 0).wait_recv()
            sums = jnp.dot(rows, wgu[place], preferred_element_type=F32)
            cols = pl.ds(pl.multiple_of(2 * HB * mod(z_hi + place, 4), 2 * HB), 2 * HB)
            for n, k in enumerate(places):
                terms[k, :, cols] = sums[ROWS * n:ROWS * (n + 1)]
        if 0 in places:
            down_along()

    gather(acts, at_y, ag_ssem, ag_rsem, FB, gate_up, weights_begun)

    def for_z(k, s):
        return terms[mod(y - z - k, 8), :, pl.ds(s * HALF, HALF)]

    both = scatter(for_z, at_z, rz_ssem, rz_rsem, rz_send, rz_recv)
    for b in range(NB):
        gate = both[b // 2][:, 2 * HB * (b % 2):2 * HB * (b % 2) + HB]
        up = both[b // 2][:, 2 * HB * (b % 2) + HB:2 * HB * (b % 2 + 1)]
        hid[0, :, pl.ds(HB * b, HB)] = (gate / (F32(1.0) + jnp.exp(-gate)) * up).astype(BF16)

    def down(places):
        if 0 in places:
            own[2].wait()

            @pl.when(c == 0)
            def _():
                for k in (1, 3, 2):
                    weight_c(k, 1).wait_recv()

        rows = jnp.concatenate([hid[k] for k in places], 0)
        total = None
        for b in range(NB):
            term = jnp.dot(rows[:, HB * b:HB * (b + 1)], wd[mod(b - z_hi, 4)], preferred_element_type=F32)
            total = term if total is None else total + term
        for n, k in enumerate(places):
            terms[k] = total[ROWS * n:ROWS * (n + 1)]

    def hand_down():
        @pl.when(c == 1)
        def _():
            for k in (1, 3, 2):
                for to in (1, 3, 2):
                    weight_x(k, to, 1).wait_recv()
                weight_c(k, 1).start()

    gather(hid, at_z, hg_ssem, hg_rsem, NB * HB, down, hand_down)

    def for_y(k, s):
        return terms[mod(z - y - k, 8), :, pl.ds(s * HALF, HALF)]

    feed = scatter(for_y, at_y, ry_ssem, ry_rsem, ry_send, ry_recv)
    for i in range(8):
        relay[pl.ds(i, ROWS, stride=8), :] = feed[i // 4][:, HD * (i % 4):HD * (i % 4 + 1)]
    f_send[...] = relay[...].astype(BF16).reshape(N, ROWS, HD)

    me = tile_of(z)
    a2 = [
        remote(f_send.at[mod(z + k, 8)], f_recv.at[me], a2_ssem.at[k - 1], a2_rsem.at[k - 1], at_z(k)) for k in far_first
    ]
    for copy in a2:
        copy.start()
    f_recv[me] = f_send[z]
    for copy in a2:
        copy.wait_recv()
    for e in range(N):
        mix = jnp.concatenate([mixed[pl.ds(QH * r + 8 * e, 8), :] for r in range(R)], 0)
        natural[pl.ds(ROWS * e, ROWS), :] = mix + f_recv[e].astype(F32)
    for e in range(N):
        for i in range(8):
            out_ref[:, pl.ds(FB * e + HD * i, HD)] = natural[pl.ds(ROWS * e + i, R, stride=8), :].astype(BF16)

    for copy in a1 + a2 + sent:
        copy.wait_send()

    for k in (1, 2, 3):
        for i in range(2):
            weight_z(k, i).wait_send()
        for to in (1, 2, 3):
            weight_x(k, to, 0).wait_send()
        weight_c(k, 0).wait_send()

    @pl.when(c == 1)
    def _():
        for k in (1, 2, 3):
            weight_z(k, 2).wait_send()
            for to in (1, 2, 3):
                weight_x(k, to, 1).wait_send()
            weight_c(k, 1).wait_send()


def per_device(q, ck, cv, nk, nv, lengths, residual, gain, gate, up, down):
    vmem = pl.BlockSpec(memory_space=pltpu.VMEM)
    hbm = pl.BlockSpec(memory_space=pl.ANY)
    dma = pltpu.SemaphoreType.DMA
    return pl.pallas_call(
        kernel,
        out_shape=jax.ShapeDtypeStruct((R, QH * HD), BF16),
        in_specs=[hbm] * 11,
        out_specs=vmem,
        scratch_shapes=[
            pltpu.SMEM((R,), jnp.int32),
            pltpu.VMEM((R, QH, HD), BF16),
            pltpu.VMEM((R, L, KVH * HD), BF16),
            pltpu.VMEM((R, L, KVH * HD), BF16),
            pltpu.VMEM((R, KVH * HD), BF16),
            pltpu.VMEM((R, KVH * HD), BF16),
            pltpu.VMEM((R, QH * HD), BF16),
            pltpu.VMEM((QH, HD), F32),
            pltpu.VMEM((NB, FB, 2 * HB), BF16),
            pltpu.VMEM((NB, HB, FB), BF16),
            pltpu.VMEM((R * QH, L), F32),
            pltpu.VMEM((R * QH, HD), F32),
            pltpu.VMEM((R * QH, HD), F32),
            pltpu.VMEM((N, ROWS, HD), BF16),
            pltpu.VMEM((N, ROWS, HD), BF16),
            pltpu.VMEM((N * ROWS, HD), F32),
            pltpu.VMEM((N, ROWS, FB), BF16),
            pltpu.VMEM((N, ROWS, FB), F32),
            pltpu.VMEM((N, ROWS, FB), BF16),
            pltpu.VMEM((N, ROWS, FB), BF16),
            pltpu.VMEM((N, ROWS, NB * HB), BF16),
            pltpu.VMEM((N, ROWS, FB), BF16),
            pltpu.VMEM((N, ROWS, FB), BF16),
            pltpu.VMEM((N, ROWS, HD), BF16),
            pltpu.VMEM((N, ROWS, HD), BF16),
            dma((8,)), dma((3,)),
            dma((3, 3)), dma((3, 3)),
            dma((3, 3, 2)), dma((3, 3, 2)),
            dma((3, 2)), dma((3, 2)),
            dma((7,)), dma((7,)),
            dma((12,)), dma((12,)),
            dma((14,)), dma((14,)),
            dma((12,)), dma((12,)),
            dma((14,)), dma((14,)),
            dma((7,)), dma((7,)),
        ],
        compiler_params=pltpu.CompilerParams(
            collective_id=0, has_side_effects=True, vmem_limit_bytes=60 * 1024 * 1024
        ),
        cost_estimate=pl.CostEstimate(flops=1_400_000_000, bytes_accessed=5_000_000, transcendentals=100_000),
    )(lengths, q, ck, cv, nk, nv, residual, gain.reshape(QH, HD), gate, up, down)


def solution(mesh):
    rows = ("pair", "role", "shard")
    return jax.shard_map(
        per_device,
        mesh=mesh,
        in_specs=(
            P(rows, None, None), P(rows, None, None), P(rows, None, None), P(rows, None), P(rows, None), P(rows),
            P(rows, None), P(), P("role", "shard"), P("role", "shard"), P("shard", "role"),
        ),
        out_specs=P(rows, None),
        check_vma=False,
    )
```

```python
import jax
import jax.numpy as jnp
from jax import lax
from jax.experimental import pallas as pl
from jax.experimental.pallas import tpu as pltpu
from jax.sharding import PartitionSpec as P

MESH = pl.DeviceIdType.MESH
F32 = jnp.float32
BF16 = jnp.bfloat16
R = 6
HD = 128
QH = 64
KVH = 4
GRP = QH // KVH
L = 128
N = 8
ROWS = R * N
FB = 1024
HB = 128
NB = 4
HALF = FB // 2


def mod(a, n):
    return lax.rem(a + 4 * n, n)


def kernel(
    len_hbm, q_hbm, ck_hbm, cv_hbm, nk_hbm, nv_hbm, res_hbm, gain_hbm, gate_hbm, up_hbm, down_hbm,
    out_ref,
    len_ref, q_ref, ck, cv, nk_ref, nv_ref, res_ref, gain_ref, wgu, wd, scores, mixed, natural, n_send, n_recv, relay,
    acts, terms, rz_send, rz_recv, hid, ry_send, ry_recv, f_send, f_recv,
    local_sem, own_sem, wz_ssem, wz_rsem, wx_ssem, wx_rsem, wc_ssem, wc_rsem, a1_ssem, a1_rsem, ag_ssem, ag_rsem,
    rz_ssem, rz_rsem, hg_ssem, hg_rsem, ry_ssem, ry_rsem, a2_ssem, a2_rsem,
):
    pair, role, shard = lax.axis_index("pair"), lax.axis_index("role"), lax.axis_index("shard")
    x, c = pair // 2, lax.rem(pair, 2)
    z_hi, y = shard // 8, lax.rem(shard, 8)
    z = z_hi * 2 + role

    def at_z(k):
        to = mod(z + k, 8)
        return (pair, lax.rem(to, 2), (to // 2) * 8 + y)

    def at_y(k):
        return (pair, role, z_hi * 8 + mod(y + k, 8))

    def at_x(k):
        return (mod(x + k, 4) * 2 + c, role, shard)

    sibling = (x * 2 + (1 - c), role, shard)

    def remote(src, dst, ssem, rsem, to):
        return pltpu.make_async_remote_copy(
            src_ref=src, dst_ref=dst, send_sem=ssem, recv_sem=rsem, device_id=to, device_id_type=MESH
        )

    operands = []
    for i, (src, dst) in enumerate((
        (q_hbm, q_ref), (ck_hbm, ck), (len_hbm, len_ref), (cv_hbm, cv), (nk_hbm, nk_ref), (nv_hbm, nv_ref), (res_hbm, res_ref), (gain_hbm, gain_ref),
    )):
        copy = pltpu.make_async_copy(src, dst, local_sem.at[i])
        copy.start()
        operands.append(copy)
    quarter = pl.ds(pl.multiple_of(z_hi * FB, FB), FB)
    own = []
    for i, (src, dst) in enumerate((
        (gate_hbm.at[quarter, :], wgu.at[0, :, pl.ds(0, HB)]),
        (up_hbm.at[quarter, :], wgu.at[0, :, pl.ds(HB, HB)]),
        (down_hbm.at[:, quarter], wd.at[0]),
    )):
        copy = pltpu.make_async_copy(src, dst, own_sem.at[i])
        copy.start()
        own.append(copy)

    barrier = pltpu.get_barrier_semaphore()

    def greet(to):
        pl.semaphore_signal(barrier, inc=1, device_id=to, device_id_type=MESH)

    for k in range(1, 8):
        greet(at_z(k))
    for k in (1, 2, 6, 7):
        greet(at_y(k))

    for k in range(1, 4):
        greet(at_x(k))
    greet(sibling)
    pl.semaphore_wait(barrier, 15)

    p = c * 4 + x
    part = pl.ds(pl.multiple_of(p * 128, 128), 128)
    part_d = pl.ds(pl.multiple_of(x * 32, 32), 32)

    def weight_z(k, i):
        q_to = mod(z_hi + k, 4)
        rows = pl.ds(pl.multiple_of(q_to * FB + p * 128, 128), 128)
        cols = pl.ds(pl.multiple_of(q_to * FB, FB), FB)
        src, dst = (
            (gate_hbm.at[rows, :], wgu.at[4 - k, part, pl.ds(0, HB)]),
            (up_hbm.at[rows, :], wgu.at[4 - k, part, pl.ds(HB, HB)]),
            (down_hbm.at[part_d, cols], wd.at[4 - k, part_d, :]),
        )[i]
        return remote(src, dst, wz_ssem.at[k - 1, i], wz_rsem.at[k - 1, i], (pair, role, q_to * 8 + y))

    def weight_x(k, to, i):
        ref = (wgu.at[4 - k, part, :], wd.at[4 - k, part_d, :])[i]
        return remote(ref, ref, wx_ssem.at[k - 1, to - 1, i], wx_rsem.at[k - 1, to - 1, i], at_x(to))

    for k in (1, 3):
        weight_z(k, 0).start()
        weight_z(k, 1).start()

    def weight_c(k, i):
        ref = (
            wgu.at[4 - k, pl.ds(pl.multiple_of(c * 512, 512), 512), :],
            wd.at[4 - k],
        )[i]
        return remote(ref, ref, wc_ssem.at[k - 1, i], wc_rsem.at[k - 1, i], sibling)

    for copy in operands[:2]:
        copy.wait()
    for r in range(R):
        for k in range(KVH):
            scores[pl.ds(QH * r + GRP * k, GRP), :] = lax.dot_general(
                q_ref[r, pl.ds(GRP * k, GRP), :], ck[r, :, pl.ds(HD * k, HD)],
                (((1,), (1,)), ((), ())), preferred_element_type=F32,
            )
    for copy in operands[2:]:
        copy.wait()
    for i in range(QH):
        mixed[pl.ds(i, R, stride=QH), :] = res_ref[:, pl.ds(HD * i, HD)].astype(F32)
    scale = F32(1.0) / jnp.sqrt(F32(HD))
    slot = lax.broadcasted_iota(jnp.int32, (QH, L), 1)
    for r in range(R):
        rows = pl.ds(QH * r, QH)
        keys = [jnp.broadcast_to(nk_ref[pl.ds(r, 1), pl.ds(HD * k, HD)].astype(F32), (GRP, HD)) for k in range(KVH)]
        vals = [jnp.broadcast_to(nv_ref[pl.ds(r, 1), pl.ds(HD * k, HD)].astype(F32), (GRP, HD)) for k in range(KVH)]
        own_score = jnp.sum(q_ref[r].astype(F32) * jnp.concatenate(keys, 0), axis=1, keepdims=True) * scale
        valid = slot < len_ref[r]
        kept = jnp.where(valid, scores[rows, :] * scale, F32(-1e30))
        top = jnp.maximum(jnp.max(kept, axis=1, keepdims=True), own_score)
        weights = jnp.where(valid, jnp.exp(kept - top), F32(0.0))
        own_weight = jnp.exp(own_score - top)
        total = jnp.sum(weights, axis=1, keepdims=True) + own_weight
        low = weights.astype(BF16)
        summed = jnp.concatenate(
            [
                jnp.dot(low[GRP * k:GRP * (k + 1)], cv[r, :, pl.ds(HD * k, HD)], preferred_element_type=F32)
                for k in range(KVH)
            ], 0,
        )
        summed = summed + own_weight.astype(BF16).astype(F32) * jnp.concatenate(vals, 0)
        mix = mixed[rows, :] + summed / total
        mixed[rows, :] = mix
        mean = jnp.sum(jnp.sum(mix * mix, axis=1, keepdims=True), axis=0, keepdims=True) * F32(1.0 / (QH * HD))
        natural[rows, :] = mix * lax.rsqrt(mean + F32(1e-5)) * gain_ref[...]

    for e in range(N):
        n_send[e] = jnp.concatenate([natural[pl.ds(QH * r + 8 * e, 8), :] for r in range(R)], 0).astype(BF16)

    def tile_of(at):
        return lax.rem(at, 2) * 4 + at // 2

    far_first = (4, 3, 5, 2, 6, 1, 7)
    a1 = [
        remote(n_send.at[tile_of(mod(z + k, 8))], n_recv.at[z], a1_ssem.at[k - 1], a1_rsem.at[k - 1], at_z(k))
        for k in far_first
    ]
    for copy in a1:
        copy.start()
    n_recv[z] = n_send[tile_of(z)]

    weight_z(2, 0).start()
    weight_z(2, 1).start()
    for k in (1, 3):
        weight_z(k, 0).wait_recv()
        weight_z(k, 1).wait_recv()
        for to in (2, 1, 3):
            weight_x(k, to, 0).start()

    for copy in a1:
        copy.wait_recv()
    relay[...] = n_recv[...].reshape(N * ROWS, HD).astype(F32)
    acts[0] = jnp.concatenate([relay[pl.ds(i, ROWS, stride=8), :] for i in range(8)], 1).astype(BF16)

    sent = []

    def push(*args):
        copy = remote(*args)
        copy.start()
        sent.append(copy)
        return copy

    def gather(buf, at, ssem, rsem, width, visit, begun):
        half = width // 2
        cols = [pl.ds(0, half), pl.ds(half, half)]
        two = {}
        for i in range(2):
            for way, k in enumerate((2, 6)):
                s = i if way == 0 else 1 - i
                n = 2 * way + s
                two[way, s] = push(buf.at[0, :, cols[s]], buf.at[k, :, cols[s]], ssem.at[n], rsem.at[n], at(k))
        one = [push(buf.at[0], buf.at[k], ssem.at[4 + n], rsem.at[4 + n], at(k)) for n, k in enumerate((1, 7))]
        begun()
        four, three = [], {}
        for i in range(2):
            for way, k in enumerate((2, 6)):
                s = i if way == 0 else 1 - i
                two[way, s].wait_recv()
                if i == 0:
                    n = 6 + way
                    four.append(push(buf.at[k, :, cols[s]], buf.at[4, :, cols[s]], ssem.at[n], rsem.at[n], at(k)))
                n = 8 + 2 * way + s
                to, place = ((1, 3), (7, 5))[way]
                three[way, s] = push(buf.at[k, :, cols[s]], buf.at[place, :, cols[s]], ssem.at[n], rsem.at[n], at(to))
        visit((0, 2, 6))
        for copy in one:
            copy.wait_recv()
        visit((1, 7))
        for copy in list(three.values()) + four:
            copy.wait_recv()
        visit((3, 5, 4))

    def scatter(term, at, ssem, rsem, sbuf, rbuf):
        cols = [pl.ds(0, HALF), pl.ds(HALF, HALF)]

        def send(value, place, s, n, k):
            sbuf[place, :, cols[s]] = value.astype(BF16)
            ref = sbuf.at[place, :, cols[s]]
            return push(ref, rbuf.at[place, :, cols[s]], ssem.at[n], rsem.at[n], at(k))

        four = [send(term(4, s), 4, s, s, (2, 6)[s]) for s in range(2)]
        three = {}
        for i in range(2):
            for way in range(2):
                s = 1 - i if way == 0 else i
                three[way, s] = send(term((3, 5)[way], s), (3, 5)[way], s, 2 + 2 * way + s, (1, 7)[way])
        one = [send(term(k, s), k, s, 6 + 2 * way + s, k) for way, k in enumerate((1, 7)) for s in range(2)]
        two = []
        for i in range(2):
            for way, k in enumerate((2, 6)):
                s = 1 - i if way == 0 else i
                value = term(k, s)
                three[way, s].wait_recv()
                value = value + rbuf[(3, 5)[way], :, cols[s]].astype(F32)
                if i == 1:
                    four[s].wait_recv()
                    value = value + rbuf[4, :, cols[s]].astype(F32)
                two.append(send(value, k, s, 10 + 2 * way + s, k))
        for copy in one + two:
            copy.wait_recv()
        out = []
        for s in range(2):
            value = term(0, s)
            for k in (1, 7, 2, 6):
                value = value + rbuf[k, :, cols[s]].astype(F32)
            out.append(value)
        return out

    def down_along():
        @pl.when(c == 1)
        def _():
            for k in (1, 3, 2):
                weight_z(k, 2).wait_recv()
                for to in (2, 1, 3):
                    weight_x(k, to, 1).start()

    def weights_begun():
        @pl.when(c == 1)
        def _():
            for k in (1, 3, 2):
                weight_z(k, 2).start()

        weight_z(2, 0).wait_recv()
        weight_z(2, 1).wait_recv()
        for to in (2, 1, 3):
            weight_x(2, to, 0).start()

    def gate_up(places):
        if 0 in places:
            own[0].wait()
            own[1].wait()

            for k in (1, 3, 2):
                for to in (1, 3, 2):
                    weight_x(k, to, 0).wait_recv()
                weight_c(k, 0).start()

        rows = jnp.concatenate([acts[k] for k in places], 0)
        for place in (0, 3, 1, 2):
            if 0 in places and place:
                weight_c(4 - place, 0).wait_recv()
            sums = jnp.dot(rows, wgu[place], preferred_element_type=F32)
            cols = pl.ds(pl.multiple_of(2 * HB * mod(z_hi + place, 4), 2 * HB), 2 * HB)
            for n, k in enumerate(places):
                terms[k, :, cols] = sums[ROWS * n:ROWS * (n + 1)]
        if 0 in places:
            down_along()

    gather(acts, at_y, ag_ssem, ag_rsem, FB, gate_up, weights_begun)

    def for_z(k, s):
        return terms[mod(y - z - k, 8), :, pl.ds(s * HALF, HALF)]

    both = scatter(for_z, at_z, rz_ssem, rz_rsem, rz_send, rz_recv)
    for b in range(NB):
        gate = both[b // 2][:, 2 * HB * (b % 2):2 * HB * (b % 2) + HB]
        up = both[b // 2][:, 2 * HB * (b % 2) + HB:2 * HB * (b % 2 + 1)]
        hid[0, :, pl.ds(HB * b, HB)] = (gate / (F32(1.0) + jnp.exp(-gate)) * up).astype(BF16)

    def down(places):
        if 0 in places:
            own[2].wait()

            @pl.when(c == 0)
            def _():
                for k in (1, 3, 2):
                    weight_c(k, 1).wait_recv()

        rows = jnp.concatenate([hid[k] for k in places], 0)
        total = None
        for b in range(NB):
            term = jnp.dot(rows[:, HB * b:HB * (b + 1)], wd[mod(b - z_hi, 4)], preferred_element_type=F32)
            total = term if total is None else total + term
        for n, k in enumerate(places):
            terms[k] = total[ROWS * n:ROWS * (n + 1)]

    def hand_down():
        @pl.when(c == 1)
        def _():
            for k in (1, 3, 2):
                for to in (1, 3, 2):
                    weight_x(k, to, 1).wait_recv()
                weight_c(k, 1).start()

    gather(hid, at_z, hg_ssem, hg_rsem, NB * HB, down, hand_down)

    def for_y(k, s):
        return terms[mod(z - y - k, 8), :, pl.ds(s * HALF, HALF)]

    feed = scatter(for_y, at_y, ry_ssem, ry_rsem, ry_send, ry_recv)
    for i in range(8):
        relay[pl.ds(i, ROWS, stride=8), :] = feed[i // 4][:, HD * (i % 4):HD * (i % 4 + 1)]
    f_send[...] = relay[...].astype(BF16).reshape(N, ROWS, HD)

    me = tile_of(z)
    a2 = [
        remote(f_send.at[mod(z + k, 8)], f_recv.at[me], a2_ssem.at[k - 1], a2_rsem.at[k - 1], at_z(k)) for k in far_first
    ]
    for copy in a2:
        copy.start()
    f_recv[me] = f_send[z]
    for copy in a2:
        copy.wait_recv()
    for e in range(N):
        mix = jnp.concatenate([mixed[pl.ds(QH * r + 8 * e, 8), :] for r in range(R)], 0)
        natural[pl.ds(ROWS * e, ROWS), :] = mix + f_recv[e].astype(F32)
    for e in range(N):
        for i in range(8):
            out_ref[:, pl.ds(FB * e + HD * i, HD)] = natural[pl.ds(ROWS * e + i, R, stride=8), :].astype(BF16)

    for copy in a1 + a2 + sent:
        copy.wait_send()

    for k in (1, 2, 3):
        for i in range(2):
            weight_z(k, i).wait_send()
        for to in (1, 2, 3):
            weight_x(k, to, 0).wait_send()
        weight_c(k, 0).wait_send()

    @pl.when(c == 1)
    def _():
        for k in (1, 2, 3):
            weight_z(k, 2).wait_send()
            for to in (1, 2, 3):
                weight_x(k, to, 1).wait_send()
            weight_c(k, 1).wait_send()


def per_device(q, ck, cv, nk, nv, lengths, residual, gain, gate, up, down):
    vmem = pl.BlockSpec(memory_space=pltpu.VMEM)
    hbm = pl.BlockSpec(memory_space=pl.ANY)
    dma = pltpu.SemaphoreType.DMA
    return pl.pallas_call(
        kernel,
        out_shape=jax.ShapeDtypeStruct((R, QH * HD), BF16),
        in_specs=[hbm] * 11,
        out_specs=vmem,
        scratch_shapes=[
            pltpu.SMEM((R,), jnp.int32),
            pltpu.VMEM((R, QH, HD), BF16),
            pltpu.VMEM((R, L, KVH * HD), BF16),
            pltpu.VMEM((R, L, KVH * HD), BF16),
            pltpu.VMEM((R, KVH * HD), BF16),
            pltpu.VMEM((R, KVH * HD), BF16),
            pltpu.VMEM((R, QH * HD), BF16),
            pltpu.VMEM((QH, HD), F32),
            pltpu.VMEM((NB, FB, 2 * HB), BF16),
            pltpu.VMEM((NB, HB, FB), BF16),
            pltpu.VMEM((R * QH, L), F32),
            pltpu.VMEM((8 * QH, HD), F32),
            pltpu.VMEM((R * QH + 16, HD), F32),
            pltpu.VMEM((N, ROWS, HD), BF16),
            pltpu.VMEM((N, ROWS, HD), BF16),
            pltpu.VMEM((N * ROWS, HD), F32),
            pltpu.VMEM((N, ROWS, FB), BF16),
            pltpu.VMEM((N, ROWS, FB), F32),
            pltpu.VMEM((N, ROWS, FB), BF16),
            pltpu.VMEM((N, ROWS, FB), BF16),
            pltpu.VMEM((N, ROWS, NB * HB), BF16),
            pltpu.VMEM((N, ROWS, FB), BF16),
            pltpu.VMEM((N, ROWS, FB), BF16),
            pltpu.VMEM((N, ROWS, HD), BF16),
            pltpu.VMEM((N, ROWS, HD), BF16),
            dma((8,)), dma((3,)),
            dma((3, 3)), dma((3, 3)),
            dma((3, 3, 2)), dma((3, 3, 2)),
            dma((3, 2)), dma((3, 2)),
            dma((7,)), dma((7,)),
            dma((12,)), dma((12,)),
            dma((14,)), dma((14,)),
            dma((12,)), dma((12,)),
            dma((14,)), dma((14,)),
            dma((7,)), dma((7,)),
        ],
        compiler_params=pltpu.CompilerParams(
            collective_id=0, has_side_effects=True, vmem_limit_bytes=60 * 1024 * 1024
        ),
        cost_estimate=pl.CostEstimate(flops=1_400_000_000, bytes_accessed=5_000_000, transcendentals=100_000),
    )(lengths, q, ck, cv, nk, nv, residual, gain.reshape(QH, HD), gate, up, down)


def solution(mesh):
    rows = ("pair", "role", "shard")
    return jax.shard_map(
        per_device,
        mesh=mesh,
        in_specs=(
            P(rows, None, None), P(rows, None, None), P(rows, None, None), P(rows, None), P(rows, None), P(rows),
            P(rows, None), P(), P("role", "shard"), P("role", "shard"), P("shard", "role"),
        ),
        out_specs=P(rows, None),
        check_vma=False,
    )
```
